256 devices in a mesh: blk: 128 (over z, x, y), grp: 2 (over core).
Axes of the slice: x: 4, y: 4, z: 8, core: 2. Of those that a mesh axis runs over, the one named last changes fastest.
Arguments:
- emission: float32 [8192, 32, 128], P('blk'), may hold values from 0.05 to 2
- positions: float32 [3, 8192, 128], P(None, 'blk'), may hold values from 0 to 6
- patch_area: float32 [8192, 128], P('blk'), may hold values from 0.03 to 0.3
- facing: float32 [8192, 128], P('blk'), may hold values from 0.2 to 1
- albedo_class: int32 [8192, 128], P('blk'), may hold values from 0 to 7
- albedo_table: float32 [8], replicated, may hold values from 0.1 to 0.7
- fetch_block: int32 [32768], P('blk'), may hold values from 0 to 63
- pair_rows: int32 [163840], P(('blk', 'grp')), may hold values from 0 to 63
- pair_slots: int32 [163840], P(('blk', 'grp')), may hold values from 0 to 255
- pair_code: int32 [163840], P(('blk', 'grp')), may hold values from 0 to 131071
Outputs:
- radiosity: float32 [8192, 32, 128], P('blk')
The draws below stay inside these ranges and needn't reach their ends.
Inputs may be any that keep to these rules, and one draw needn't show every extreme that they name: `fetch_block`: slot s of index b of blk names a block owned by index s // 2 of blk.
All inputs are finite; a program needn't handle non-finite values.
Results may differ from the reference program's by a relative error of at most 0.0003.
Values may be sent and summed in bfloat16 or wider, within the bound.
No kernel may reach another device: no remote copies, remote signals or barrier semaphores. Data moves between devices by JAX's collectives and lax.ppermute only.
A program may use at most 128 MiB of HBM per device.

```python
import math
import jax
import jax.numpy as jnp
from jax import lax

BLOCK = 128
H = 32
NCLASS = 8
SWEEPS = 2
PER_OWNER = 2
BLK_DEV = 64
PAIRS_DEV = 640
SLOTS = 256
NBLOCKS = 8192
PAIRS = 163840
N_BLK = 128
N_GRP = 2


def set_ends(array, stream_key, least, top_value):
    spot = [jax.random.randint(jax.random.fold_in(stream_key, axis), (), 0, length) for axis, length in enumerate(array.shape)]
    widest = array.shape.index(max(array.shape))
    neighbour = spot[:widest] + [(spot[widest] + 1) % array.shape[widest]] + spot[widest + 1:]
    return array.at[tuple(spot)].set(least).at[tuple(neighbour)].set(top_value)


def levels(rng, extent, split, smallest, largest):
    gain = 1.0
    for axis_at, parts in split:
        heights = jax.random.uniform(jax.random.fold_in(jax.random.fold_in(rng, 6), axis_at), (parts,), jnp.float32, smallest / len(split), largest / len(split))
        gain = gain * jnp.repeat(jnp.exp(heights), extent[axis_at] // parts).reshape((-1,) + (1,) * (len(extent) - 1 - axis_at))
    return gain


def setup_inputs(seed: int = 0) -> dict:
    arg_keys = jax.random.split(jax.random.key(seed), 11)
    return {
        "emission": jnp.clip(jnp.exp(math.log(2.0) - 3.6888794 * jax.random.uniform(arg_keys[0], (NBLOCKS, H, BLOCK), jnp.float32) ** levels(arg_keys[0], (NBLOCKS, H, BLOCK), ((0, 128),), -0.2, 0.2)), 0.05, 2.0),
        "positions": jnp.clip(6.0 * jax.random.uniform(arg_keys[1], (3, NBLOCKS, BLOCK), jnp.float32) ** levels(arg_keys[1], (3, NBLOCKS, BLOCK), ((1, 128),), -0.2, 0.2), 0.0, 6.0),
        "patch_area": jnp.clip(jnp.exp(math.log(0.3) - 2.3025852 * jax.random.uniform(arg_keys[2], (NBLOCKS, BLOCK), jnp.float32) ** levels(arg_keys[2], (NBLOCKS, BLOCK), ((0, 128),), -0.2, 0.2)), 0.03, 0.3),
        "facing": jnp.clip(jnp.exp(math.log(1.0) - 1.609438 * jax.random.uniform(arg_keys[3], (NBLOCKS, BLOCK), jnp.float32) ** levels(arg_keys[3], (NBLOCKS, BLOCK), ((0, 128),), -0.2, 0.2)), 0.2, 1.0),
        "albedo_class": set_ends(jax.random.randint(arg_keys[4], (NBLOCKS, BLOCK), 0, NCLASS), jax.random.fold_in(arg_keys[4], 1), 0, NCLASS - 1).astype(jnp.int32),
        "albedo_table": jnp.clip(jax.random.uniform(arg_keys[5], (NCLASS,), jnp.float32, 0.1, 0.7), 0.1, 0.7),
        "fetch_block": set_ends(jax.random.randint(arg_keys[6], (N_BLK * SLOTS,), 0, BLK_DEV), jax.random.fold_in(arg_keys[6], 1), 0, BLK_DEV - 1).astype(jnp.int32),
        "pair_rows": set_ends(jax.random.randint(arg_keys[7], (PAIRS,), 0, BLK_DEV), jax.random.fold_in(arg_keys[7], 1), 0, BLK_DEV - 1).astype(jnp.int32),
        "pair_slots": set_ends(jax.random.randint(arg_keys[8], (PAIRS,), 0, SLOTS), jax.random.fold_in(arg_keys[8], 1), 0, SLOTS - 1).astype(jnp.int32),
        "pair_code": set_ends(jax.random.randint(arg_keys[9], (PAIRS,), 0, 131072), jax.random.fold_in(arg_keys[9], 1), 0, 131071).astype(jnp.int32),
    }


def visible(pair_kind):
    patch_ids = jnp.arange(BLOCK, dtype=jnp.int32)
    hashed = pair_kind.astype(jnp.int32)[:, None, None] * (BLOCK * BLOCK) + patch_ids[None, :, None] * BLOCK + patch_ids[None, None, :]
    hashed = hashed * 747796405
    hashed = hashed ^ jnp.left_shift(hashed, 13)
    hashed = hashed ^ lax.shift_right_logical(hashed, jnp.full_like(hashed, 17))
    hashed = hashed ^ jnp.left_shift(hashed, 5)
    return (lax.shift_right_logical(hashed, jnp.full_like(hashed, 7)) & 1).astype(jnp.float32)


def build_tiles(geo_near, geo_far, pair_kind):
    distance_sq = jnp.zeros((geo_near.shape[0], BLOCK, BLOCK), jnp.float32)
    for component in range(3):
        offset = geo_near[:, component, :, None] - geo_far[:, component, None, :]
        distance_sq = distance_sq + offset * offset
    soften = geo_near[:, 3, :, None] + geo_far[:, 3, None, :]
    facing_pair = geo_near[:, 4, :, None] * geo_far[:, 4, None, :]
    return (visible(pair_kind) * facing_pair / (math.pi * (distance_sq + soften))).astype(jnp.bfloat16)


def reference(emission, positions, patch_area, facing, albedo_class, albedo_table, fetch_block, pair_rows, pair_slots, pair_code):
    geometry = jnp.stack([positions[0], positions[1], positions[2], patch_area, facing], axis=1)
    class_ids = jnp.arange(NCLASS, dtype=jnp.int32)
    albedo = jnp.sum(jnp.where(albedo_class[..., None] == class_ids, albedo_table, jnp.float32(0.0)), axis=-1)
    slot_owner = jnp.arange(SLOTS, dtype=jnp.int32) // PER_OWNER
    slot_block = slot_owner[None, :] * BLK_DEV + fetch_block.reshape(N_BLK, SLOTS).astype(jnp.int32)
    device_total = N_BLK * N_GRP
    row_table = pair_rows.reshape(device_total, PAIRS_DEV)
    slot_table = pair_slots.reshape(device_total, PAIRS_DEV)
    kind_table = pair_code.reshape(device_total, PAIRS_DEV)
    device_ids = jnp.arange(device_total, dtype=jnp.int32)
    radiance = emission
    for sweep_number in range(SWEEPS):
        exitance = (patch_area[:, None, :] * radiance).astype(jnp.bfloat16)

        def accumulate(irradiance, inputs):
            device_id, row_ids, slot_ids, kind_ids = inputs
            blk_row = device_id // N_GRP
            near_blocks = blk_row * BLK_DEV + row_ids
            far_blocks = slot_block[blk_row][slot_ids]
            form_tile = build_tiles(geometry[near_blocks], geometry[far_blocks], kind_ids).astype(jnp.float32)
            to_rows = jnp.einsum('bpq,bhq->bhp', form_tile, exitance[far_blocks].astype(jnp.float32))
            to_cols = jnp.einsum('bpq,bhp->bhq', form_tile, exitance[near_blocks].astype(jnp.float32))
            irradiance = irradiance.at[near_blocks].add(to_rows).at[far_blocks].add(to_cols)
            return irradiance, None

        irradiance = lax.scan(accumulate, jnp.zeros(emission.shape, jnp.float32), (device_ids, row_table, slot_table, kind_table))[0]
        radiance = emission + albedo[:, None, :] * irradiance
    return radiance
```

```python
import math

import jax
import jax.numpy as jnp
import numpy as np
from jax import lax
from jax.experimental import pallas as pl
from jax.experimental.pallas import tpu as pltpu
from jax.sharding import PartitionSpec as P

BLOCK = 128
NCLASS = 8
HASH = 747796405
FEATURES = 32
UNROLL = 16
DEPTH = 8
VMEM = 48 * 1024 * 1024

SPARE = 64 | (128 << 7)


def hash_pattern():
    at = (np.arange(BLOCK * BLOCK, dtype=np.uint64) * HASH) & 0xFFFFFFFF
    odd = (at >> 2) ^ (at >> 6) ^ (at >> 7) ^ (at >> 11)
    word = (((at >> 14) << 21) + ((odd & 1) << 31)) & 0xFFFFFFFF
    return word.astype(np.uint32).astype(np.int32).reshape(BLOCK, BLOCK)


def row_of(word):
    return word & 127


def slot_of(word):
    return lax.shift_right_logical(word, jnp.int32(7)) & 255


def list_kernel(words_ref, list_ref, steps_ref):
    total = words_ref.shape[0]

    def take(turn, count):
        for j in range(8):
            word = words_ref[turn * 8 + j]
            list_ref[count] = word
            count = count + 1 - (lax.shift_right_logical(word, jnp.int32(6)) & 1)
        return count

    count = lax.fori_loop(0, total // 8, take, jnp.int32(0))
    for j in range(UNROLL):
        list_ref[count + j] = jnp.int32(SPARE)
    steps_ref[0] = jnp.maximum((count + UNROLL - 1) // UNROLL, 1)


def pair_list(words):
    total = words.shape[0]
    smem = pl.BlockSpec(memory_space=pltpu.SMEM)
    return pl.pallas_call(
        list_kernel,
        out_shape=(
            jax.ShapeDtypeStruct((total + UNROLL,), jnp.int32),
            jax.ShapeDtypeStruct((1,), jnp.int32),
        ),
        in_specs=[smem],
        out_specs=(smem, smem),
        cost_estimate=pl.CostEstimate(flops=10_000_000, bytes_accessed=10_000_000, transcendentals=0),
    )(words)


def encode(acc, out_ref):
    def one(slot, carry):
        value = acc[slot]
        top = jnp.max(value, axis=0, keepdims=True)
        exponent = jnp.ceil(jnp.log2(jnp.maximum(top, 1e-30)))
        level = jnp.minimum(jnp.round(value * jnp.exp2(15.0 - exponent)), 32767.0).astype(jnp.int32)
        biased = exponent.astype(jnp.int32) + 128
        places = lax.broadcasted_iota(jnp.int32, value.shape, 0)
        mark = jnp.where(places < 8, lax.shift_right_logical(biased, jnp.minimum(places, 8)) & 1, 0)
        out_ref[slot] = (level ^ -mark).astype(jnp.int16)
        return carry

    lax.fori_loop(0, out_ref.shape[0], one, 0, unroll=4)


def decode(code):
    code = code.astype(jnp.int32)
    head = code[:8]
    places = lax.broadcasted_iota(jnp.int32, head.shape, 0)
    bits = jnp.where(head < 0, jnp.left_shift(jnp.ones_like(head), places), 0).astype(jnp.float32)
    biased = jnp.sum(bits, axis=0, keepdims=True)
    level = code ^ lax.shift_right_arithmetic(code, jnp.full_like(code, 31))
    return level.astype(jnp.float32) * jnp.exp2(biased - (128.0 + 15.0))


def tile_copy(tiles_ref, held, sems, step, out):
    buffer = lax.rem(step, DEPTH)
    away = tiles_ref.at[pl.ds(step * UNROLL, UNROLL)]
    here = held.at[buffer]
    source, target = (here, away) if out else (away, here)
    return pltpu.make_async_copy(source, target, sems.at[buffer])


def build_kernel(
    list_ref, steps_ref, pattern_ref, near_ref, far_ref, ex_ref, tiles_ref, out_ref, acc, held, sems
):
    steps = steps_ref[0]
    acc[...] = jnp.zeros_like(acc)

    def turn(step, carry):
        buffer = lax.rem(step, DEPTH)

        @pl.when(step >= DEPTH)
        def _():
            tile_copy(tiles_ref, held, sems, step - DEPTH, True).wait()

        for j in range(UNROLL):
            word = list_ref[step * UNROLL + j]
            row, slot = row_of(word) & 63, slot_of(word)
            shift = jnp.left_shift(lax.shift_right_logical(word, jnp.int32(15)) * jnp.int32(HASH), 21)
            scaled = jnp.dot(near_ref[row], far_ref[slot & 127], preferred_element_type=jnp.float32)
            mixed = pattern_ref[...] + shift
            mixed = mixed ^ jnp.left_shift(mixed, 5)
            tile = jnp.where(mixed < 0, pl.reciprocal(scaled, approx=True), 0.0).astype(jnp.bfloat16)
            held[buffer, j] = tile
            acc[slot] += jnp.dot(ex_ref[row], tile, preferred_element_type=jnp.float32)
        tile_copy(tiles_ref, held, sems, step, True).start()
        return carry

    lax.fori_loop(0, steps, turn, 0)
    encode(acc, out_ref)

    def drain(step, carry):
        tile_copy(tiles_ref, held, sems, step, True).wait()
        return carry

    lax.fori_loop(jnp.maximum(steps - DEPTH, 0), steps, drain, 0)


def stream(steps, tiles_ref, held, sems, use):
    def fetch(step, carry):
        tile_copy(tiles_ref, held, sems, step, False).start()
        return carry

    lax.fori_loop(0, jnp.minimum(steps, DEPTH - 1), fetch, 0)

    def turn(step, carry):
        @pl.when(step + DEPTH - 1 < steps)
        def _():
            fetch(step + DEPTH - 1, 0)

        tile_copy(tiles_ref, held, sems, step, False).wait()
        use(step, lax.rem(step, DEPTH))
        return carry

    lax.fori_loop(0, steps, turn, 0)


def columns_kernel(list_ref, steps_ref, tiles_ref, ex_ref, out_ref, acc, held, sems):
    acc[...] = jnp.zeros_like(acc)

    def use(step, buffer):
        for j in range(UNROLL):
            word = list_ref[step * UNROLL + j]
            row, slot = row_of(word) & 63, slot_of(word)
            acc[slot] += jnp.dot(ex_ref[row], held[buffer, j], preferred_element_type=jnp.float32)

    stream(steps_ref[0], tiles_ref, held, sems, use)
    encode(acc, out_ref)


def rows_kernel(list_ref, steps_ref, tiles_ref, ex_ref, out_ref, held, sems):
    out_ref[...] = jnp.zeros_like(out_ref)

    def use(step, buffer):
        for j in range(UNROLL):
            word = list_ref[step * UNROLL + j]
            row, slot = row_of(word), slot_of(word) & 127
            out_ref[row] += lax.dot_general(
                ex_ref[slot], held[buffer, j], (((1,), (1,)), ((), ())),
                preferred_element_type=jnp.float32,
            )

    stream(steps_ref[0], tiles_ref, held, sems, use)


SMEM_SPEC = pl.BlockSpec(memory_space=pltpu.SMEM)
VMEM_SPEC = pl.BlockSpec(memory_space=pltpu.VMEM)
ANY_SPEC = pl.BlockSpec(memory_space=pl.ANY)
HELD = pltpu.VMEM((DEPTH, UNROLL, BLOCK, BLOCK), jnp.bfloat16)
SEMS = pltpu.SemaphoreType.DMA((DEPTH,))


def build(pairs, steps, pattern, near, far, exitance, pair_max):
    slots, hours = far.shape[0], exitance.shape[1]
    return pl.pallas_call(
        build_kernel,
        in_specs=[SMEM_SPEC] * 2 + [VMEM_SPEC] * 4,
        out_specs=[ANY_SPEC, VMEM_SPEC],
        out_shape=[
            jax.ShapeDtypeStruct((pair_max, BLOCK, BLOCK), jnp.bfloat16),
            jax.ShapeDtypeStruct((slots, hours, BLOCK), jnp.int16),
        ],
        scratch_shapes=[pltpu.VMEM((slots + 1, hours, BLOCK), jnp.float32), HELD, SEMS],
        compiler_params=pltpu.CompilerParams(vmem_limit_bytes=VMEM),
        cost_estimate=pl.CostEstimate(
            flops=20_000_000_000, bytes_accessed=60_000_000, transcendentals=10_000_000
        ),
    )(pairs, steps, pattern, near, far, exitance)


def columns(pairs, steps, tiles, exitance, slots):
    hours = exitance.shape[1]
    return pl.pallas_call(
        columns_kernel,
        in_specs=[SMEM_SPEC] * 2 + [ANY_SPEC, VMEM_SPEC],
        out_specs=VMEM_SPEC,
        out_shape=jax.ShapeDtypeStruct((slots, hours, BLOCK), jnp.int16),
        scratch_shapes=[pltpu.VMEM((slots + 1, hours, BLOCK), jnp.float32), HELD, SEMS],
        compiler_params=pltpu.CompilerParams(vmem_limit_bytes=VMEM),
        cost_estimate=pl.CostEstimate(flops=10_000_000_000, bytes_accessed=40_000_000, transcendentals=0),
    )(pairs, steps, tiles, exitance)


def rows(pairs, steps, tiles, fetched, row_blocks):
    hours = fetched.shape[1]
    return pl.pallas_call(
        rows_kernel,
        in_specs=[SMEM_SPEC] * 2 + [ANY_SPEC, VMEM_SPEC],
        out_specs=VMEM_SPEC,
        out_shape=jax.ShapeDtypeStruct((row_blocks + 1, hours, BLOCK), jnp.float32),
        scratch_shapes=[HELD, SEMS],
        compiler_params=pltpu.CompilerParams(vmem_limit_bytes=VMEM),
        cost_estimate=pl.CostEstimate(flops=10_000_000_000, bytes_accessed=40_000_000, transcendentals=0),
    )(pairs, steps, tiles, fetched)


def gather_into(acc, mine_ref, other_ref, got_ref, got_other_ref, asked_ref, asked_other_ref):
    blocks = acc.shape[0]
    acc[...] = mine_ref[:blocks] + other_ref[:blocks]

    def add(at, carry):
        for asked, got in ((asked_ref, got_ref), (asked_other_ref, got_other_ref)):
            acc[asked[at]] += decode(got[at])
        return carry

    lax.fori_loop(0, got_ref.shape[0], add, 0, unroll=4)


def middle_kernel(
    asked_ref, asked_other_ref, mine_ref, other_ref, got_ref, got_other_ref,
    emission_ref, albedo_ref, area_ref, ex_ref, send_ref, acc,
):
    gather_into(acc, mine_ref, other_ref, got_ref, got_other_ref, asked_ref, asked_other_ref)
    ex_ref[...] = (area_ref[...] * (emission_ref[...] + albedo_ref[...] * acc[...])).astype(jnp.bfloat16)

    def put(at, carry):
        send_ref[at] = ex_ref[asked_ref[at]]
        return carry

    lax.fori_loop(0, send_ref.shape[0], put, 0, unroll=8)


def last_kernel(
    asked_ref, asked_other_ref, mine_ref, other_ref, got_ref, got_other_ref,
    emission_ref, albedo_ref, out_ref, acc,
):
    gather_into(acc, mine_ref, other_ref, got_ref, got_other_ref, asked_ref, asked_other_ref)
    out_ref[...] = emission_ref[...] + albedo_ref[...] * acc[...]


def update(kernel, asked, asked_other, arrays, out_shape):
    smem, vmem = pl.BlockSpec(memory_space=pltpu.SMEM), pl.BlockSpec(memory_space=pltpu.VMEM)
    blocks, hours, block = arrays[4].shape
    return pl.pallas_call(
        kernel,
        in_specs=[smem, smem] + [vmem] * len(arrays),
        out_specs=jax.tree.map(lambda _: vmem, out_shape),
        out_shape=out_shape,
        scratch_shapes=[pltpu.VMEM((blocks, hours, block), jnp.float32)],
        compiler_params=pltpu.CompilerParams(vmem_limit_bytes=VMEM),
    )(asked, asked_other, *arrays)


def three_parts(value):
    top = lax.reduce_precision(value, 8, 7)
    value = value - top
    middle = lax.reduce_precision(value, 8, 7)
    return top, middle, lax.reduce_precision(value - middle, 8, 7)


def features(geometry, near):
    x, y, z = (geometry[:, i] - 3.0 for i in range(3))
    unit = (math.pi if near else 1.0) / geometry[:, 4]
    norm = unit * (x * x + y * y + z * z + geometry[:, 3])
    if near:
        terms = (norm, unit, -2.0 * unit * x, -2.0 * unit * y, -2.0 * unit * z)
        order = (0, 0, 1, 1, 0, 2)
    else:
        terms = (unit, norm, unit * x, unit * y, unit * z)
        order = (0, 1, 0, 1, 2, 0)
    columns_ = []
    for term in terms:
        parts = three_parts(term)
        columns_ += [parts[i] for i in order]
    columns_ += [jnp.zeros_like(x)] * (FEATURES - len(columns_))
    return jnp.stack(columns_, axis=1).astype(jnp.bfloat16)


def local(
    emission, positions, patch_area, facing, albedo_class, albedo_table, fetch_block,
    pair_rows, pair_slots, pair_code,
):
    blocks, hours = emission.shape[:2]
    owners = lax.axis_size("blk")
    core = lax.axis_index("grp")

    def exchange(array):
        return lax.all_to_all(array, "blk", split_axis=0, concat_axis=0, tiled=True)

    def swap(array):
        return lax.ppermute(array, "grp", [(0, 1), (1, 0)])

    wanted = lax.dynamic_slice_in_dim(fetch_block.reshape(owners, 2), core, 1, axis=1)
    asked = exchange(wanted.reshape(owners, 1, 1)).reshape(owners)
    asked_other = swap(asked)
    mine = jnp.stack([pair_rows, pair_slots, pair_code])
    pair_row, pair_slot, code = jnp.concatenate([mine, swap(mine)], axis=1)
    skip = (pair_slot & 1) ^ core
    words = pair_row | (skip << 6) | ((pair_slot >> 1) << 7) | jnp.left_shift(code, 15)
    pairs, steps = pair_list(words)

    geometry = jnp.stack([positions[0], positions[1], positions[2], patch_area, facing], axis=1)
    near = features(geometry, True).transpose(0, 2, 1)
    geometry_slots = exchange(geometry.reshape(blocks, 1, 5 * BLOCK)[asked])
    exitance = (patch_area[:, None, :] * emission).astype(jnp.bfloat16)
    send = exitance[asked]
    send, geometry_slots = lax.optimization_barrier((send, geometry_slots))
    far = features(geometry_slots.reshape(owners, 5, BLOCK), False)

    class_ids = jnp.arange(NCLASS, dtype=jnp.int32)
    albedo = jnp.sum(
        jnp.where(albedo_class[..., None] == class_ids, albedo_table, jnp.float32(0.0)), axis=-1
    )[:, None, :]
    area = patch_area[:, None, :]

    fetched = exchange(send)
    tiles, back = build(
        pairs, steps, jnp.asarray(hash_pattern()), near, far, exitance, 2 * pair_rows.shape[0]
    )
    back, fetched = lax.optimization_barrier((back, fetched))
    got = exchange(back)
    to_rows = rows(pairs, steps, tiles, fetched, blocks)
    to_rows_other = swap(to_rows)
    exitance, send = update(
        middle_kernel, asked, asked_other,
        (to_rows, to_rows_other, got, swap(got), emission, albedo, area),
        [
            jax.ShapeDtypeStruct((blocks, hours, BLOCK), jnp.bfloat16),
            jax.ShapeDtypeStruct((owners, hours, BLOCK), jnp.bfloat16),
        ],
    )

    fetched = exchange(send)
    back = columns(pairs, steps, tiles, exitance, owners)
    back, fetched = lax.optimization_barrier((back, fetched))
    got = exchange(back)
    to_rows = rows(pairs, steps, tiles, fetched, blocks)
    to_rows_other = swap(to_rows)
    return update(
        last_kernel, asked, asked_other,
        (to_rows, to_rows_other, got, swap(got), emission, albedo),
        jax.ShapeDtypeStruct((blocks, hours, BLOCK), jnp.float32),
    )


def solution(mesh):
    in_specs = (
        P("blk", None, None),
        P(None, "blk", None),
        P("blk", None),
        P("blk", None),
        P("blk", None),
        P(),
        P("blk"),
        P(("blk", "grp")),
        P(("blk", "grp")),
        P(("blk", "grp")),
    )
    out_specs = P("blk", None, None)
    return jax.shard_map(local, mesh=mesh, in_specs=in_specs, out_specs=out_specs, check_vma=False)
```

```python
import math

import jax
import jax.numpy as jnp
import numpy as np
from jax import lax
from jax.experimental import pallas as pl
from jax.experimental.pallas import tpu as pltpu
from jax.sharding import PartitionSpec as P

BLOCK = 128
NCLASS = 8
HASH = 747796405
FEATURES = 32
UNROLL = 16
DEPTH = 8
VMEM = 60 * 1024 * 1024
SMEM_SPEC = pl.BlockSpec(memory_space=pltpu.SMEM)
VMEM_SPEC = pl.BlockSpec(memory_space=pltpu.VMEM)
ANY_SPEC = pl.BlockSpec(memory_space=pl.ANY)

SPARE = 64 | (128 << 7)


def hash_pattern():
    at = (np.arange(BLOCK * BLOCK, dtype=np.uint64) * HASH) & 0xFFFFFFFF
    odd = (at >> 2) ^ (at >> 6) ^ (at >> 7) ^ (at >> 11)
    word = (((at >> 14) << 21) + ((odd & 1) << 31)) & 0xFFFFFFFF
    return word.astype(np.uint32).astype(np.int32).reshape(BLOCK, BLOCK)


def row_of(word):
    return word & 127


def slot_of(word):
    return lax.shift_right_logical(word, jnp.int32(7)) & 255


def list_kernel(words_ref, list_ref, steps_ref):
    total = words_ref.shape[0]

    def take(turn, count):
        for j in range(8):
            word = words_ref[turn * 8 + j]
            list_ref[count] = word
            count = count + 1 - (lax.shift_right_logical(word, jnp.int32(6)) & 1)
        return count

    count = lax.fori_loop(0, total // 8, take, jnp.int32(0))
    for j in range(UNROLL):
        list_ref[count + j] = jnp.int32(SPARE)
    steps_ref[0] = jnp.maximum((count + UNROLL - 1) // UNROLL, 1)


def pair_list(words):
    total = words.shape[0]
    return pl.pallas_call(
        list_kernel,
        out_shape=(
            jax.ShapeDtypeStruct((total + UNROLL,), jnp.int32),
            jax.ShapeDtypeStruct((1,), jnp.int32),
        ),
        in_specs=[SMEM_SPEC],
        out_specs=(SMEM_SPEC, SMEM_SPEC),
        cost_estimate=pl.CostEstimate(flops=10_000_000, bytes_accessed=10_000_000, transcendentals=0),
    )(words)


def encode(acc, out_ref):
    def one(slot, carry):
        value = acc[slot]
        top = jnp.max(value, axis=0, keepdims=True)
        exponent = jnp.ceil(jnp.log2(jnp.maximum(top, 1e-30)))
        level = jnp.minimum(jnp.round(value * jnp.exp2(15.0 - exponent)), 32767.0).astype(jnp.int32)
        biased = exponent.astype(jnp.int32) + 128
        places = lax.broadcasted_iota(jnp.int32, value.shape, 0)
        mark = jnp.where(places < 8, lax.shift_right_logical(biased, jnp.minimum(places, 8)) & 1, 0)
        out_ref[slot] = (level ^ -mark).astype(jnp.int16)
        return carry

    lax.fori_loop(0, out_ref.shape[0], one, 0, unroll=4)


def decode(code):
    code = code.astype(jnp.int32)
    head = code[:8]
    places = lax.broadcasted_iota(jnp.int32, head.shape, 0)
    bits = jnp.where(head < 0, jnp.left_shift(jnp.ones_like(head), places), 0).astype(jnp.float32)
    biased = jnp.sum(bits, axis=0, keepdims=True)
    level = code ^ lax.shift_right_arithmetic(code, jnp.full_like(code, 31))
    return level.astype(jnp.float32) * jnp.exp2(biased - (128.0 + 15.0))


def tile_copy(tiles_ref, held, sems, step, out):
    buffer = lax.rem(step, DEPTH)
    away = tiles_ref.at[pl.ds(step * UNROLL, UNROLL)]
    here = held.at[buffer]
    source, target = (here, away) if out else (away, here)
    return pltpu.make_async_copy(source, target, sems.at[buffer])


def build_kernel(
    list_ref, steps_ref, pattern_ref, near_ref, far_ref, ex_ref, tiles_ref, out_ref, acc, held, sems
):
    steps = steps_ref[0]
    acc[...] = jnp.zeros_like(acc)

    def turn(step, carry):
        buffer = lax.rem(step, DEPTH)

        @pl.when(step >= DEPTH)
        def _():
            tile_copy(tiles_ref, held, sems, step - DEPTH, True).wait()

        for j in range(UNROLL):
            word = list_ref[step * UNROLL + j]
            row, slot = row_of(word) & 63, slot_of(word)
            shift = jnp.left_shift(lax.shift_right_logical(word, jnp.int32(15)) * jnp.int32(HASH), 21)
            scaled = jnp.dot(near_ref[row], far_ref[slot & 127], preferred_element_type=jnp.float32)
            mixed = pattern_ref[...] + shift
            mixed = mixed ^ jnp.left_shift(mixed, 5)
            tile = jnp.where(mixed < 0, pl.reciprocal(scaled, approx=True), 0.0).astype(jnp.bfloat16)
            held[buffer, j] = tile
            acc[slot] += jnp.dot(ex_ref[row], tile, preferred_element_type=jnp.float32)
        tile_copy(tiles_ref, held, sems, step, True).start()
        return carry

    lax.fori_loop(0, steps, turn, 0)
    encode(acc, out_ref)

    def drain(step, carry):
        tile_copy(tiles_ref, held, sems, step, True).wait()
        return carry

    lax.fori_loop(jnp.maximum(steps - DEPTH, 0), steps, drain, 0)


def stream(steps, tiles_ref, held, sems, use):
    def fetch(step, carry):
        tile_copy(tiles_ref, held, sems, step, False).start()
        return carry

    lax.fori_loop(0, jnp.minimum(steps, DEPTH - 1), fetch, 0)

    def turn(step, carry):
        @pl.when(step + DEPTH - 1 < steps)
        def _():
            fetch(step + DEPTH - 1, 0)

        tile_copy(tiles_ref, held, sems, step, False).wait()
        use(step, lax.rem(step, DEPTH))
        return carry

    lax.fori_loop(0, steps, turn, 0)


def columns_kernel(list_ref, steps_ref, tiles_ref, ex_ref, out_ref, acc, held, sems):
    acc[...] = jnp.zeros_like(acc)

    def use(step, buffer):
        for j in range(UNROLL):
            word = list_ref[step * UNROLL + j]
            row, slot = row_of(word) & 63, slot_of(word)
            acc[slot] += jnp.dot(ex_ref[row], held[buffer, j], preferred_element_type=jnp.float32)

    stream(steps_ref[0], tiles_ref, held, sems, use)
    encode(acc, out_ref)


def rows_kernel(list_ref, steps_ref, tiles_ref, ex_ref, out_ref, held, sems):
    out_ref[...] = jnp.zeros_like(out_ref)

    def use(step, buffer):
        for j in range(UNROLL):
            word = list_ref[step * UNROLL + j]
            row, slot = row_of(word), slot_of(word) & 127
            out_ref[row] += lax.dot_general(
                ex_ref[slot], held[buffer, j], (((1,), (1,)), ((), ())),
                preferred_element_type=jnp.float32,
            )

    stream(steps_ref[0], tiles_ref, held, sems, use)


HELD = pltpu.VMEM((DEPTH, UNROLL, BLOCK, BLOCK), jnp.bfloat16)
SEMS = pltpu.SemaphoreType.DMA((DEPTH,))


def build(pairs, steps, pattern, near, far, exitance, pair_max):
    slots, hours = far.shape[0], exitance.shape[1]
    return pl.pallas_call(
        build_kernel,
        in_specs=[SMEM_SPEC] * 2 + [VMEM_SPEC] * 4,
        out_specs=[ANY_SPEC, VMEM_SPEC],
        out_shape=[
            jax.ShapeDtypeStruct((pair_max, BLOCK, BLOCK), jnp.bfloat16),
            jax.ShapeDtypeStruct((slots, hours, BLOCK), jnp.int16),
        ],
        scratch_shapes=[pltpu.VMEM((slots + 1, hours, BLOCK), jnp.float32), HELD, SEMS],
        compiler_params=pltpu.CompilerParams(vmem_limit_bytes=VMEM),
        cost_estimate=pl.CostEstimate(
            flops=20_000_000_000, bytes_accessed=60_000_000, transcendentals=10_000_000
        ),
    )(pairs, steps, pattern, near, far, exitance)


def columns(pairs, steps, tiles, exitance, slots):
    hours = exitance.shape[1]
    return pl.pallas_call(
        columns_kernel,
        in_specs=[SMEM_SPEC] * 2 + [ANY_SPEC, VMEM_SPEC],
        out_specs=VMEM_SPEC,
        out_shape=jax.ShapeDtypeStruct((slots, hours, BLOCK), jnp.int16),
        scratch_shapes=[pltpu.VMEM((slots + 1, hours, BLOCK), jnp.float32), HELD, SEMS],
        compiler_params=pltpu.CompilerParams(vmem_limit_bytes=VMEM),
        cost_estimate=pl.CostEstimate(flops=10_000_000_000, bytes_accessed=40_000_000, transcendentals=0),
    )(pairs, steps, tiles, exitance)


def rows(pairs, steps, tiles, fetched, row_blocks):
    hours = fetched.shape[1]
    return pl.pallas_call(
        rows_kernel,
        in_specs=[SMEM_SPEC] * 2 + [ANY_SPEC, VMEM_SPEC],
        out_specs=VMEM_SPEC,
        out_shape=jax.ShapeDtypeStruct((row_blocks + 1, hours, BLOCK), jnp.float32),
        scratch_shapes=[HELD, SEMS],
        compiler_params=pltpu.CompilerParams(vmem_limit_bytes=VMEM),
        cost_estimate=pl.CostEstimate(flops=10_000_000_000, bytes_accessed=40_000_000, transcendentals=0),
    )(pairs, steps, tiles, fetched)


def gather_into(acc, mine_ref, other_ref, got_ref, got_other_ref, asked_ref, asked_other_ref):
    blocks = acc.shape[0]
    acc[...] = mine_ref[:blocks] + other_ref[:blocks]

    def add(at, carry):
        for asked, got in ((asked_ref, got_ref), (asked_other_ref, got_other_ref)):
            acc[asked[at, 0]] += decode(got[at])
        return carry

    lax.fori_loop(0, got_ref.shape[0], add, 0, unroll=4)


def middle_kernel(
    asked_ref, asked_other_ref, mine_ref, other_ref, got_ref, got_other_ref,
    emission_ref, albedo_ref, area_ref, ex_ref, send_ref, acc,
):
    gather_into(acc, mine_ref, other_ref, got_ref, got_other_ref, asked_ref, asked_other_ref)
    ex_ref[...] = (area_ref[...] * (emission_ref[...] + albedo_ref[...] * acc[...])).astype(jnp.bfloat16)

    def put(at, carry):
        send_ref[at] = ex_ref[asked_ref[at, 0]]
        return carry

    lax.fori_loop(0, send_ref.shape[0], put, 0, unroll=8)


def last_kernel(
    asked_ref, asked_other_ref, mine_ref, other_ref, got_ref, got_other_ref,
    emission_ref, albedo_ref, out_ref, acc,
):
    gather_into(acc, mine_ref, other_ref, got_ref, got_other_ref, asked_ref, asked_other_ref)
    out_ref[...] = emission_ref[...] + albedo_ref[...] * acc[...]


def update(kernel, asked, asked_other, arrays, out_shape):
    blocks, hours, block = arrays[4].shape
    return pl.pallas_call(
        kernel,
        in_specs=[SMEM_SPEC] * 2 + [VMEM_SPEC] * len(arrays),
        out_specs=jax.tree.map(lambda _: VMEM_SPEC, out_shape),
        out_shape=out_shape,
        scratch_shapes=[pltpu.VMEM((blocks, hours, block), jnp.float32)],
        compiler_params=pltpu.CompilerParams(vmem_limit_bytes=VMEM // 4),
    )(asked, asked_other, *arrays)


def ask_kernel(core_ref, fetch_ref, out_ref):
    core = core_ref[0]
    for owner in range(out_ref.shape[0]):
        out_ref[owner] = jnp.full((1, BLOCK), fetch_ref[2 * owner + core], jnp.int32)


def ask(core, fetch_block, owners):
    return pl.pallas_call(
        ask_kernel,
        in_specs=[SMEM_SPEC] * 2,
        out_specs=VMEM_SPEC,
        out_shape=jax.ShapeDtypeStruct((owners, 1, BLOCK), jnp.int32),
    )(core.reshape(1), fetch_block)


def place_kernel(asked_ref, positions_ref, area_ref, facing_ref, out_ref):
    def put(at, carry):
        block = pl.ds(asked_ref[at, 0], 1)
        for i in range(3):
            out_ref[at, :, i * BLOCK : (i + 1) * BLOCK] = positions_ref[i, block, :]
        out_ref[at, :, 3 * BLOCK : 4 * BLOCK] = area_ref[block, :]
        out_ref[at, :, 4 * BLOCK : 5 * BLOCK] = facing_ref[block, :]
        return carry

    lax.fori_loop(0, out_ref.shape[0], put, 0, unroll=8)


def place(asked, positions, patch_area, facing):
    return pl.pallas_call(
        place_kernel,
        in_specs=[SMEM_SPEC] + [VMEM_SPEC] * 3,
        out_specs=VMEM_SPEC,
        out_shape=jax.ShapeDtypeStruct((asked.shape[0], 1, 5 * BLOCK), jnp.float32),
        compiler_params=pltpu.CompilerParams(vmem_limit_bytes=VMEM),
    )(asked, positions, patch_area, facing)


def first_kernel(asked_ref, emission_ref, area_ref, ex_ref, send_ref):
    ex_ref[...] = (area_ref[...] * emission_ref[...]).astype(jnp.bfloat16)

    def put(at, carry):
        send_ref[at] = ex_ref[asked_ref[at, 0]]
        return carry

    lax.fori_loop(0, send_ref.shape[0], put, 0, unroll=8)


def first(asked, emission, area):
    blocks, hours, block = emission.shape
    return pl.pallas_call(
        first_kernel,
        in_specs=[SMEM_SPEC] + [VMEM_SPEC] * 2,
        out_specs=[VMEM_SPEC] * 2,
        out_shape=[
            jax.ShapeDtypeStruct((blocks, hours, block), jnp.bfloat16),
            jax.ShapeDtypeStruct((asked.shape[0], hours, block), jnp.bfloat16),
        ],
        compiler_params=pltpu.CompilerParams(vmem_limit_bytes=VMEM),
        cost_estimate=pl.CostEstimate(flops=1_000_000, bytes_accessed=4_000_000, transcendentals=0),
    )(asked, emission, area)


def factor_rows(x, y, z, area, facing, near):
    x, y, z = x - 3.0, y - 3.0, z - 3.0
    unit = (math.pi if near else 1.0) / facing
    norm = unit * (x * x + y * y + z * z + area)
    if near:
        terms = (norm, unit, -2.0 * unit * x, -2.0 * unit * y, -2.0 * unit * z)
        order = (0, 0, 1, 1, 0, 2)
    else:
        terms = (unit, norm, unit * x, unit * y, unit * z)
        order = (0, 1, 0, 1, 2, 0)
    found = []
    for term in terms:
        parts = []
        for _ in range(3):
            part = term.astype(jnp.bfloat16).astype(jnp.float32)
            parts.append(part)
            term = term - part
        found += [parts[i] for i in order]
    return found + [jnp.zeros_like(x)] * (FEATURES - len(found))


def factor_blocks(read, count, turned, near, put):
    def group(at, carry):
        for i, feature in enumerate(factor_rows(*read(pl.ds(pl.multiple_of(at * 8, 8), 8)), near)):
            turned[8 * i : 8 * i + 8, :] = feature
        for i in range(8):
            put(at * 8 + i, turned[pl.ds(i, FEATURES, stride=8), :])
        return carry

    lax.fori_loop(0, count // 8, group, 0)


def near_kernel(positions_ref, area_ref, facing_ref, out_ref, turned):
    def read(at):
        return [positions_ref[i, at, :] for i in range(3)] + [area_ref[at, :], facing_ref[at, :]]

    def put(at, block):
        out_ref[at] = block.T.astype(jnp.bfloat16)

    factor_blocks(read, out_ref.shape[0], turned, True, put)


def far_kernel(geometry_ref, out_ref, turned):
    def read(at):
        return [geometry_ref[at, 0, i * BLOCK : (i + 1) * BLOCK] for i in range(5)]

    def put(at, block):
        out_ref[at] = block.astype(jnp.bfloat16)

    factor_blocks(read, out_ref.shape[0], turned, False, put)


def factors(kernel, arrays, shape):
    return pl.pallas_call(
        kernel,
        in_specs=[VMEM_SPEC] * len(arrays),
        out_specs=VMEM_SPEC,
        out_shape=jax.ShapeDtypeStruct(shape, jnp.bfloat16),
        scratch_shapes=[pltpu.VMEM((8 * FEATURES, BLOCK), jnp.float32)],
        compiler_params=pltpu.CompilerParams(vmem_limit_bytes=VMEM),
        cost_estimate=pl.CostEstimate(flops=10_000_000, bytes_accessed=8_000_000, transcendentals=0),
    )(*arrays)


def local(
    emission, positions, patch_area, facing, albedo_class, albedo_table, fetch_block,
    pair_rows, pair_slots, pair_code,
):
    blocks, hours = emission.shape[:2]
    owners = lax.axis_size("blk")
    core = lax.axis_index("grp")

    def exchange(array):
        return lax.all_to_all(array, "blk", split_axis=0, concat_axis=0, tiled=True)

    def swap(array):
        return lax.ppermute(array, "grp", [(0, 1), (1, 0)])

    asked = exchange(ask(core, fetch_block, owners)).reshape(owners, BLOCK)
    mine = jnp.stack([pair_rows, pair_slots, pair_code])
    pair_row, pair_slot, code = jnp.concatenate([mine, swap(mine)], axis=1)
    skip = (pair_slot & 1) ^ core
    words = pair_row | (skip << 6) | ((pair_slot >> 1) << 7) | jnp.left_shift(code, 15)
    pairs, steps = pair_list(words)
    area = patch_area[:, None, :]

    near = factors(near_kernel, (positions, patch_area, facing), (blocks, BLOCK, FEATURES))
    asked, near, pairs, steps = lax.optimization_barrier((asked, near, pairs, steps))
    geometry = exchange(place(asked, positions, patch_area, facing))
    asked_other = swap(asked)
    exitance, send = first(asked, emission, area)
    send, geometry = lax.optimization_barrier((send, geometry))
    far = factors(far_kernel, (geometry,), (owners, FEATURES, BLOCK))

    class_ids = jnp.arange(NCLASS, dtype=jnp.int32)
    albedo = jnp.sum(
        jnp.where(albedo_class[..., None] == class_ids, albedo_table, jnp.float32(0.0)), axis=-1
    )[:, None, :]

    fetched = exchange(send)
    tiles, back = build(
        pairs, steps, jnp.asarray(hash_pattern()), near, far, exitance, 2 * pair_rows.shape[0]
    )
    got = exchange(back)
    to_rows = rows(pairs, steps, tiles, fetched, blocks)
    to_rows_other = swap(to_rows)
    exitance, send = update(
        middle_kernel, asked, asked_other,
        (to_rows, to_rows_other, got, swap(got), emission, albedo, area),
        [
            jax.ShapeDtypeStruct((blocks, hours, BLOCK), jnp.bfloat16),
            jax.ShapeDtypeStruct((owners, hours, BLOCK), jnp.bfloat16),
        ],
    )

    fetched = exchange(send)
    back = columns(pairs, steps, tiles, exitance, owners)
    got = exchange(back)
    to_rows = rows(pairs, steps, tiles, fetched, blocks)
    to_rows_other = swap(to_rows)
    return update(
        last_kernel, asked, asked_other,
        (to_rows, to_rows_other, got, swap(got), emission, albedo),
        jax.ShapeDtypeStruct((blocks, hours, BLOCK), jnp.float32),
    )


def solution(mesh):
    in_specs = (
        P("blk", None, None),
        P(None, "blk", None),
        P("blk", None),
        P("blk", None),
        P("blk", None),
        P(),
        P("blk"),
        P(("blk", "grp")),
        P(("blk", "grp")),
        P(("blk", "grp")),
    )
    out_specs = P("blk", None, None)
    return jax.shard_map(local, mesh=mesh, in_specs=in_specs, out_specs=out_specs, check_vma=False)
```

```python
import math

import jax
import jax.numpy as jnp
import numpy as np
from jax import lax
from jax.experimental import pallas as pl
from jax.experimental.pallas import tpu as pltpu
from jax.sharding import PartitionSpec as P

BLOCK = 128
NCLASS = 8
HASH = 747796405
FEATURES = 32
UNROLL = 16
DEPTH = 8
VMEM = 60 * 1024 * 1024
SMEM_SPEC = pl.BlockSpec(memory_space=pltpu.SMEM)
VMEM_SPEC = pl.BlockSpec(memory_space=pltpu.VMEM)
ANY_SPEC = pl.BlockSpec(memory_space=pl.ANY)
HBM_SPEC = pl.BlockSpec(memory_space=pltpu.HBM)
PARTS = 4

SPARE = 64 | (128 << 7)


def hash_pattern():
    at = (np.arange(BLOCK * BLOCK, dtype=np.uint64) * HASH) & 0xFFFFFFFF
    odd = (at >> 2) ^ (at >> 6) ^ (at >> 7) ^ (at >> 11)
    word = (((at >> 14) << 21) + ((odd & 1) << 31)) & 0xFFFFFFFF
    return word.astype(np.uint32).astype(np.int32).reshape(BLOCK, BLOCK)


def row_of(word):
    return word & 127


def slot_of(word):
    return lax.shift_right_logical(word, jnp.int32(7)) & 255


def list_kernel(mine_ref, other_ref, list_ref, steps_ref):
    def take_from(words_ref):
        def take(turn, count):
            for j in range(8):
                word = words_ref[turn * 8 + j]
                list_ref[count] = word
                count = count + 1 - (lax.shift_right_logical(word, jnp.int32(6)) & 1)
            return count

        return take

    turns = mine_ref.shape[0] // 8
    count = lax.fori_loop(0, turns, take_from(mine_ref), jnp.int32(0))
    count = lax.fori_loop(0, turns, take_from(other_ref), count)
    for j in range(UNROLL):
        list_ref[count + j] = jnp.int32(SPARE)
    steps_ref[0] = jnp.maximum((count + UNROLL - 1) // UNROLL, 1)


def pair_list(mine, other):
    return pl.pallas_call(
        list_kernel,
        out_shape=(
            jax.ShapeDtypeStruct((2 * mine.shape[0] + UNROLL,), jnp.int32),
            jax.ShapeDtypeStruct((1,), jnp.int32),
        ),
        in_specs=[SMEM_SPEC] * 2,
        out_specs=(SMEM_SPEC, SMEM_SPEC),
        cost_estimate=pl.CostEstimate(flops=10_000_000, bytes_accessed=10_000_000, transcendentals=0),
    )(mine, other)


def encode(acc, out_ref):
    def one(slot, carry):
        value = acc[slot]
        top = jnp.max(value, axis=0, keepdims=True)
        exponent = jnp.ceil(jnp.log2(jnp.maximum(top, 1e-30)))
        level = jnp.minimum(jnp.round(value * jnp.exp2(15.0 - exponent)), 32767.0).astype(jnp.int32)
        biased = exponent.astype(jnp.int32) + 128
        places = lax.broadcasted_iota(jnp.int32, value.shape, 0)
        mark = jnp.where(places < 8, lax.shift_right_logical(biased, jnp.minimum(places, 8)) & 1, 0)
        out_ref[slot] = (level ^ -mark).astype(jnp.int16)
        return carry

    lax.fori_loop(0, out_ref.shape[0], one, 0, unroll=4)


def decode(code):
    code = code.astype(jnp.int32)
    head = code[:8]
    places = lax.broadcasted_iota(jnp.int32, head.shape, 0)
    bits = jnp.where(head < 0, jnp.left_shift(jnp.ones_like(head), places), 0).astype(jnp.float32)
    biased = jnp.sum(bits, axis=0, keepdims=True)
    level = code ^ lax.shift_right_arithmetic(code, jnp.full_like(code, 31))
    return level.astype(jnp.float32) * jnp.exp2(biased - (128.0 + 15.0))


def tile_copy(tiles_ref, held, sems, step, out):
    buffer = lax.rem(step, DEPTH)
    away = tiles_ref.at[pl.ds(step * UNROLL, UNROLL)]
    here = held.at[buffer]
    source, target = (here, away) if out else (away, here)
    return pltpu.make_async_copy(source, target, sems.at[buffer])


def build_kernel(
    list_ref, steps_ref, pattern_ref, near_ref, far_ref, ex_ref, tiles_ref, out_ref, acc, held, sems
):
    steps = steps_ref[0]
    acc[...] = jnp.zeros_like(acc)

    def turn(step, carry):
        buffer = lax.rem(step, DEPTH)

        @pl.when(step >= DEPTH)
        def _():
            tile_copy(tiles_ref, held, sems, step - DEPTH, True).wait()

        for j in range(UNROLL):
            word = list_ref[step * UNROLL + j]
            row, slot = row_of(word) & 63, slot_of(word)
            shift = jnp.left_shift(lax.shift_right_logical(word, jnp.int32(15)) * jnp.int32(HASH), 21)
            scaled = jnp.dot(near_ref[row], far_ref[slot & 127], preferred_element_type=jnp.float32)
            mixed = pattern_ref[...] + shift
            mixed = mixed ^ jnp.left_shift(mixed, 5)
            tile = jnp.where(mixed < 0, pl.reciprocal(scaled, approx=True), 0.0).astype(jnp.bfloat16)
            held[buffer, j] = tile
            acc[slot] += jnp.dot(ex_ref[row], tile, preferred_element_type=jnp.float32)
        tile_copy(tiles_ref, held, sems, step, True).start()
        return carry

    lax.fori_loop(0, steps, turn, 0)
    encode(acc, out_ref)

    def drain(step, carry):
        tile_copy(tiles_ref, held, sems, step, True).wait()
        return carry

    lax.fori_loop(jnp.maximum(steps - DEPTH, 0), steps, drain, 0)


def stream(steps, tiles_ref, held, sems, use):
    def fetch(step, carry):
        tile_copy(tiles_ref, held, sems, step, False).start()
        return carry

    lax.fori_loop(0, jnp.minimum(steps, DEPTH - 1), fetch, 0)

    def turn(step, carry):
        @pl.when(step + DEPTH - 1 < steps)
        def _():
            fetch(step + DEPTH - 1, 0)

        tile_copy(tiles_ref, held, sems, step, False).wait()
        use(step, lax.rem(step, DEPTH))
        return carry

    lax.fori_loop(0, steps, turn, 0)


def columns_kernel(list_ref, steps_ref, tiles_ref, ex_ref, out_ref, acc, held, sems):
    acc[...] = jnp.zeros_like(acc)

    def use(step, buffer):
        for j in range(UNROLL):
            word = list_ref[step * UNROLL + j]
            row, slot = row_of(word) & 63, slot_of(word)
            acc[slot] += jnp.dot(ex_ref[row], held[buffer, j], preferred_element_type=jnp.float32)

    stream(steps_ref[0], tiles_ref, held, sems, use)
    encode(acc, out_ref)


def rows_kernel(list_ref, steps_ref, tiles_ref, ex_ref, out_ref, held, sems):
    out_ref[...] = jnp.zeros_like(out_ref)

    def use(step, buffer):
        for j in range(UNROLL):
            word = list_ref[step * UNROLL + j]
            row, slot = row_of(word), slot_of(word) & 127
            out_ref[row] += lax.dot_general(
                ex_ref[slot], held[buffer, j], (((1,), (1,)), ((), ())),
                preferred_element_type=jnp.float32,
            )

    stream(steps_ref[0], tiles_ref, held, sems, use)


HELD = pltpu.VMEM((DEPTH, UNROLL, BLOCK, BLOCK), jnp.bfloat16)
SEMS = pltpu.SemaphoreType.DMA((DEPTH,))


def build(pairs, steps, pattern, near, far, exitance, pair_max):
    slots, hours = far.shape[0], exitance.shape[1]
    return pl.pallas_call(
        build_kernel,
        in_specs=[SMEM_SPEC] * 2 + [VMEM_SPEC] * 4,
        out_specs=[ANY_SPEC, VMEM_SPEC],
        out_shape=[
            jax.ShapeDtypeStruct((pair_max, BLOCK, BLOCK), jnp.bfloat16),
            jax.ShapeDtypeStruct((slots, hours, BLOCK), jnp.int16),
        ],
        scratch_shapes=[pltpu.VMEM((slots + 1, hours, BLOCK), jnp.float32), HELD, SEMS],
        compiler_params=pltpu.CompilerParams(vmem_limit_bytes=VMEM),
        cost_estimate=pl.CostEstimate(
            flops=20_000_000_000, bytes_accessed=60_000_000, transcendentals=10_000_000
        ),
    )(pairs, steps, pattern, near, far, exitance)


def columns(pairs, steps, tiles, exitance, slots):
    hours = exitance.shape[1]
    return pl.pallas_call(
        columns_kernel,
        in_specs=[SMEM_SPEC] * 2 + [ANY_SPEC, VMEM_SPEC],
        out_specs=VMEM_SPEC,
        out_shape=jax.ShapeDtypeStruct((slots, hours, BLOCK), jnp.int16),
        scratch_shapes=[pltpu.VMEM((slots + 1, hours, BLOCK), jnp.float32), HELD, SEMS],
        compiler_params=pltpu.CompilerParams(vmem_limit_bytes=VMEM),
        cost_estimate=pl.CostEstimate(flops=10_000_000_000, bytes_accessed=40_000_000, transcendentals=0),
    )(pairs, steps, tiles, exitance)


def rows(pairs, steps, tiles, fetched, row_blocks):
    hours = fetched.shape[1]
    return pl.pallas_call(
        rows_kernel,
        in_specs=[SMEM_SPEC] * 2 + [ANY_SPEC, VMEM_SPEC],
        out_specs=VMEM_SPEC,
        out_shape=jax.ShapeDtypeStruct((row_blocks + 1, hours, BLOCK), jnp.float32),
        scratch_shapes=[HELD, SEMS],
        compiler_params=pltpu.CompilerParams(vmem_limit_bytes=VMEM),
        cost_estimate=pl.CostEstimate(flops=10_000_000_000, bytes_accessed=40_000_000, transcendentals=0),
    )(pairs, steps, tiles, fetched)


def add_asked(acc, asked_ref, got_ref):
    def add(at, carry):
        acc[asked_ref[at, 0]] += decode(got_ref[at])
        return carry

    lax.fori_loop(0, got_ref.shape[0], add, 0, unroll=8)


def own_kernel(asked_ref, got_ref, out_ref):
    out_ref[...] = jnp.zeros_like(out_ref)
    add_asked(out_ref, asked_ref, got_ref)


def own(asked, got, blocks):
    return pl.pallas_call(
        own_kernel,
        in_specs=[SMEM_SPEC, VMEM_SPEC],
        out_specs=VMEM_SPEC,
        out_shape=jax.ShapeDtypeStruct((blocks,) + got.shape[1:], jnp.float32),
        compiler_params=pltpu.CompilerParams(vmem_limit_bytes=VMEM // 4),
        cost_estimate=pl.CostEstimate(flops=10_000_000, bytes_accessed=4_000_000, transcendentals=0),
    )(asked, got)


def middle_kernel(
    asked_ref, asked_other_ref, own_ref, got_ref, base_ref, albedo_ref, area_ref, ex_out_ref, send_ref,
    acc, ex, send, ex_sems, send_sems,
):
    acc[...] = own_ref[...]
    add_asked(acc, asked_other_ref, got_ref)
    ex[...] = (area_ref[...] * (base_ref[...] + albedo_ref[...] * acc[...])).astype(jnp.bfloat16)
    send_copies = part_copies(send, send_ref, send_sems)
    ex_copies = part_copies(ex, ex_out_ref, ex_sems)
    put_asked(asked_ref, ex, send, send_copies)
    for copy in ex_copies:
        copy.start()
    for copy in ex_copies + send_copies:
        copy.wait()


def middle(asked, asked_other, own_sum, got, base, albedo, area):
    blocks, hours, block = base.shape
    owners = asked.shape[0]
    return pl.pallas_call(
        middle_kernel,
        in_specs=[SMEM_SPEC] * 2 + [VMEM_SPEC] * 5,
        out_specs=[HBM_SPEC] * 2,
        out_shape=[
            jax.ShapeDtypeStruct((blocks, hours, block), jnp.bfloat16),
            jax.ShapeDtypeStruct((owners, hours, block), jnp.bfloat16),
        ],
        scratch_shapes=[
            pltpu.VMEM((blocks, hours, block), jnp.float32),
            pltpu.VMEM((blocks, hours, block), jnp.bfloat16),
            pltpu.VMEM((owners, hours, block), jnp.bfloat16),
            pltpu.SemaphoreType.DMA((PARTS,)),
            pltpu.SemaphoreType.DMA((PARTS,)),
        ],
        compiler_params=pltpu.CompilerParams(vmem_limit_bytes=VMEM // 4),
    )(asked, asked_other, own_sum, got, base, albedo, area)


def last_kernel(asked_other_ref, own_ref, got_ref, base_ref, albedo_ref, out_ref, acc, sems):
    acc[...] = own_ref[...]
    add_asked(acc, asked_other_ref, got_ref)
    size = acc.shape[0] // PARTS
    copies = part_copies(acc, out_ref, sems)
    for i, copy in enumerate(copies):
        part = slice(i * size, (i + 1) * size)
        acc[part] = base_ref[part] + albedo_ref[part] * acc[part]
        copy.start()
    for copy in copies:
        copy.wait()


def last(asked_other, own_sum, got, base, albedo):
    return pl.pallas_call(
        last_kernel,
        in_specs=[SMEM_SPEC] + [VMEM_SPEC] * 4,
        out_specs=HBM_SPEC,
        out_shape=jax.ShapeDtypeStruct(base.shape, jnp.float32),
        scratch_shapes=[
            pltpu.VMEM(base.shape, jnp.float32),
            pltpu.SemaphoreType.DMA((PARTS,)),
        ],
        compiler_params=pltpu.CompilerParams(vmem_limit_bytes=VMEM // 4),
    )(asked_other, own_sum, got, base, albedo)


def ask_kernel(core_ref, fetch_ref, out_ref):
    core = core_ref[0]
    for owner in range(out_ref.shape[0]):
        out_ref[owner] = jnp.full((1, BLOCK), fetch_ref[2 * owner + core], jnp.int32)


def ask(core, fetch_block, owners):
    return pl.pallas_call(
        ask_kernel,
        in_specs=[SMEM_SPEC] * 2,
        out_specs=VMEM_SPEC,
        out_shape=jax.ShapeDtypeStruct((owners, 1, BLOCK), jnp.int32),
    )(core.reshape(1), fetch_block)


def part_copies(source, target, sems):
    size = source.shape[0] // PARTS
    return [
        pltpu.make_async_copy(
            source.at[pl.ds(i * size, size)], target.at[pl.ds(i * size, size)], sems.at[i]
        )
        for i in range(PARTS)
    ]


def put_asked(asked_ref, ex_ref, send, copies):
    size = send.shape[0] // PARTS

    def put(at, carry):
        send[at] = ex_ref[asked_ref[at, 0]]
        return carry

    for i, copy in enumerate(copies):
        lax.fori_loop(i * size, (i + 1) * size, put, 0, unroll=8)
        copy.start()


def serve_kernel(
    asked_ref, positions_ref, area_ref, facing_ref, emission_ref, ex_ref, place_ref, send_ref,
    placed, send, place_sems, send_sems,
):
    def put(at, carry):
        block = pl.ds(asked_ref[at, 0], 1)
        for i in range(3):
            placed[at, :, i * BLOCK : (i + 1) * BLOCK] = positions_ref[i, block, :]
        placed[at, :, 3 * BLOCK : 4 * BLOCK] = area_ref[block, 0, :]
        placed[at, :, 4 * BLOCK : 5 * BLOCK] = facing_ref[block, :]
        return carry

    place_copies = part_copies(placed, place_ref, place_sems)
    send_copies = part_copies(send, send_ref, send_sems)
    size = placed.shape[0] // PARTS
    for i, copy in enumerate(place_copies):
        lax.fori_loop(i * size, (i + 1) * size, put, 0, unroll=8)
        copy.start()
    ex_ref[...] = (area_ref[...] * emission_ref[...]).astype(jnp.bfloat16)
    put_asked(asked_ref, ex_ref, send, send_copies)
    for copy in place_copies + send_copies:
        copy.wait()


def serve(asked, positions, area, facing, emission):
    blocks, hours, block = emission.shape
    owners = asked.shape[0]
    return pl.pallas_call(
        serve_kernel,
        in_specs=[SMEM_SPEC] + [VMEM_SPEC] * 4,
        out_specs=[VMEM_SPEC, HBM_SPEC, HBM_SPEC],
        out_shape=[
            jax.ShapeDtypeStruct((blocks, hours, block), jnp.bfloat16),
            jax.ShapeDtypeStruct((owners, 1, 5 * block), jnp.float32),
            jax.ShapeDtypeStruct((owners, hours, block), jnp.bfloat16),
        ],
        scratch_shapes=[
            pltpu.VMEM((owners, 1, 5 * block), jnp.float32),
            pltpu.VMEM((owners, hours, block), jnp.bfloat16),
            pltpu.SemaphoreType.DMA((PARTS,)),
            pltpu.SemaphoreType.DMA((PARTS,)),
        ],
        compiler_params=pltpu.CompilerParams(vmem_limit_bytes=VMEM // 4),
    )(asked, positions, area, facing, emission)


def factor_rows(x, y, z, area, facing, near):
    x, y, z = x - 3.0, y - 3.0, z - 3.0
    unit = (math.pi if near else 1.0) / facing
    norm = unit * (x * x + y * y + z * z + area)
    if near:
        terms = (norm, unit, -2.0 * unit * x, -2.0 * unit * y, -2.0 * unit * z)
        order = (0, 0, 1, 1, 0, 2)
    else:
        terms = (unit, norm, unit * x, unit * y, unit * z)
        order = (0, 1, 0, 1, 2, 0)
    found = []
    for term in terms:
        parts = []
        for _ in range(3):
            part = term.astype(jnp.bfloat16).astype(jnp.float32)
            parts.append(part)
            term = term - part
        found += [parts[i] for i in order]
    return found + [jnp.zeros_like(x)] * (FEATURES - len(found))


def factor_blocks(read, count, turned, near, put):
    def group(at, carry):
        for i, feature in enumerate(factor_rows(*read(pl.ds(pl.multiple_of(at * 8, 8), 8)), near)):
            turned[8 * i : 8 * i + 8, :] = feature
        for i in range(8):
            put(at * 8 + i, turned[pl.ds(i, FEATURES, stride=8), :])
        return carry

    lax.fori_loop(0, count // 8, group, 0)


def near_kernel(positions_ref, area_ref, facing_ref, out_ref, turned):
    def read(at):
        return [positions_ref[i, at, :] for i in range(3)] + [area_ref[at, :], facing_ref[at, :]]

    def put(at, block):
        out_ref[at] = block.T.astype(jnp.bfloat16)

    factor_blocks(read, out_ref.shape[0], turned, True, put)


def far_kernel(geometry_ref, out_ref, turned):
    def read(at):
        return [geometry_ref[at, 0, i * BLOCK : (i + 1) * BLOCK] for i in range(5)]

    def put(at, block):
        out_ref[at] = block.astype(jnp.bfloat16)

    factor_blocks(read, out_ref.shape[0], turned, False, put)


def factors(kernel, arrays, shape):
    return pl.pallas_call(
        kernel,
        in_specs=[VMEM_SPEC] * len(arrays),
        out_specs=VMEM_SPEC,
        out_shape=jax.ShapeDtypeStruct(shape, jnp.bfloat16),
        scratch_shapes=[pltpu.VMEM((8 * FEATURES, BLOCK), jnp.float32)],
        compiler_params=pltpu.CompilerParams(vmem_limit_bytes=VMEM),
        cost_estimate=pl.CostEstimate(flops=10_000_000, bytes_accessed=8_000_000, transcendentals=0),
    )(*arrays)


def local(
    emission, positions, patch_area, facing, albedo_class, albedo_table, fetch_block,
    pair_rows, pair_slots, pair_code,
):
    blocks, hours = emission.shape[:2]
    owners = lax.axis_size("blk")
    core = lax.axis_index("grp")

    def exchange(array):
        return lax.all_to_all(array, "blk", split_axis=0, concat_axis=0, tiled=True)

    def swap(array):
        return lax.ppermute(array, "grp", [(0, 1), (1, 0)])

    asked = exchange(ask(core, fetch_block, owners)).reshape(owners, BLOCK)

    def words(pair_row, pair_slot, code):
        skip = (pair_slot & 1) ^ core
        return pair_row | (skip << 6) | ((pair_slot >> 1) << 7) | jnp.left_shift(code, 15)

    lists = (pair_rows, pair_slots, pair_code)
    pairs, steps = pair_list(words(*lists), words(*map(swap, lists)))
    near = factors(near_kernel, (positions, patch_area, facing), (blocks, BLOCK, FEATURES))
    asked, near, pairs, steps = lax.optimization_barrier((asked, near, pairs, steps))

    area = patch_area[:, None, :]
    exitance, place, send = serve(asked, positions, area, facing, emission)
    geometry = exchange(place)
    send, geometry, asked, albedo_class = lax.optimization_barrier((send, geometry, asked, albedo_class))
    far = factors(far_kernel, (geometry,), (owners, FEATURES, BLOCK))
    asked_other = swap(asked)

    class_ids = jnp.arange(NCLASS, dtype=jnp.int32)
    albedo = jnp.sum(
        jnp.where(albedo_class[..., None] == class_ids, albedo_table, jnp.float32(0.0)), axis=-1
    )[:, None, :]

    fetched = exchange(send)
    tiles, back = build(
        pairs, steps, jnp.asarray(hash_pattern()), near, far, exitance, 2 * pair_rows.shape[0]
    )

    def collect(back, fetched):
        got = exchange(back)
        to_rows = rows(pairs, steps, tiles, fetched, blocks)
        base = emission + albedo * (to_rows[:blocks] + swap(to_rows)[:blocks])
        return own(asked, got, blocks), swap(got), base

    exitance, send = middle(asked, asked_other, *collect(back, fetched), albedo, area)
    fetched = exchange(send)
    back = columns(pairs, steps, tiles, exitance, owners)
    return last(asked_other, *collect(back, fetched), albedo)


def solution(mesh):
    in_specs = (
        P("blk", None, None),
        P(None, "blk", None),
        P("blk", None),
        P("blk", None),
        P("blk", None),
        P(),
        P("blk"),
        P(("blk", "grp")),
        P(("blk", "grp")),
        P(("blk", "grp")),
    )
    out_specs = P("blk", None, None)
    return jax.shard_map(local, mesh=mesh, in_specs=in_specs, out_specs=out_specs, check_vma=False)
```

```python
import math

import jax
import jax.numpy as jnp
import numpy as np
from jax import lax
from jax.experimental import pallas as pl
from jax.experimental.pallas import tpu as pltpu
from jax.sharding import PartitionSpec as P

BLOCK = 128
NCLASS = 8
HASH = 747796405
FEATURES = 32
UNROLL = 64
DEPTH = 4
VMEM = 60 * 1024 * 1024
SMEM_SPEC = pl.BlockSpec(memory_space=pltpu.SMEM)
VMEM_SPEC = pl.BlockSpec(memory_space=pltpu.VMEM)
ANY_SPEC = pl.BlockSpec(memory_space=pl.ANY)
HBM_SPEC = pl.BlockSpec(memory_space=pltpu.HBM)
PARTS = 4

SPARE = 64 | (128 << 7)


def hash_pattern():
    at = (np.arange(BLOCK * BLOCK, dtype=np.uint64) * HASH) & 0xFFFFFFFF
    odd = (at >> 2) ^ (at >> 6) ^ (at >> 7) ^ (at >> 11)
    word = (((at >> 14) << 21) + ((odd & 1) << 31)) & 0xFFFFFFFF
    return word.astype(np.uint32).astype(np.int32).reshape(BLOCK, BLOCK)


def row_of(word):
    return word & 127


def slot_of(word):
    return lax.shift_right_logical(word, jnp.int32(7)) & 255


def list_kernel(mine_ref, other_ref, list_ref, steps_ref):
    def take_from(words_ref):
        def take(turn, count):
            for j in range(8):
                word = words_ref[turn * 8 + j]
                list_ref[count] = word
                count = count + 1 - (lax.shift_right_logical(word, jnp.int32(6)) & 1)
            return count

        return take

    turns = mine_ref.shape[0] // 8
    count = lax.fori_loop(0, turns, take_from(mine_ref), jnp.int32(0))
    count = lax.fori_loop(0, turns, take_from(other_ref), count)
    for j in range(UNROLL):
        list_ref[count + j] = jnp.int32(SPARE)
    steps_ref[0] = jnp.maximum((count + UNROLL - 1) // UNROLL, 1)


def pair_list(mine, other):
    return pl.pallas_call(
        list_kernel,
        out_shape=(
            jax.ShapeDtypeStruct((2 * mine.shape[0] + UNROLL,), jnp.int32),
            jax.ShapeDtypeStruct((1,), jnp.int32),
        ),
        in_specs=[SMEM_SPEC] * 2,
        out_specs=(SMEM_SPEC, SMEM_SPEC),
        cost_estimate=pl.CostEstimate(flops=10_000_000, bytes_accessed=10_000_000, transcendentals=0),
    )(mine, other)


def encode(acc, out_ref):
    def one(slot, carry):
        value = acc[slot]
        top = jnp.max(value, axis=0, keepdims=True)
        exponent = jnp.ceil(jnp.log2(jnp.maximum(top, 1e-30)))
        level = jnp.minimum(jnp.round(value * jnp.exp2(15.0 - exponent)), 32767.0).astype(jnp.int32)
        biased = exponent.astype(jnp.int32) + 128
        places = lax.broadcasted_iota(jnp.int32, value.shape, 0)
        mark = jnp.where(places < 8, lax.shift_right_logical(biased, jnp.minimum(places, 8)) & 1, 0)
        out_ref[slot] = (level ^ -mark).astype(jnp.int16)
        return carry

    lax.fori_loop(0, out_ref.shape[0], one, 0, unroll=4)


def decode(code):
    code = code.astype(jnp.int32)
    head = code[:8]
    places = lax.broadcasted_iota(jnp.int32, head.shape, 0)
    bits = jnp.where(head < 0, jnp.left_shift(jnp.ones_like(head), places), 0).astype(jnp.float32)
    biased = jnp.sum(bits, axis=0, keepdims=True)
    level = code ^ lax.shift_right_arithmetic(code, jnp.full_like(code, 31))
    return level.astype(jnp.float32) * jnp.exp2(biased - (128.0 + 15.0))


def tile_copy(tiles_ref, held, sems, step, out):
    buffer = lax.rem(step, DEPTH)
    away = tiles_ref.at[pl.ds(step * UNROLL, UNROLL)]
    here = held.at[buffer]
    source, target = (here, away) if out else (away, here)
    return pltpu.make_async_copy(source, target, sems.at[buffer])


def build_kernel(
    list_ref, steps_ref, pattern_ref, near_ref, geometry_ref, ex_ref, tiles_ref, out_ref,
    acc, held, sems, far, turned,
):
    steps = steps_ref[0]
    far_factors(geometry_ref, far, turned)
    acc[...] = jnp.zeros_like(acc)

    def turn(step, carry):
        buffer = lax.rem(step, DEPTH)

        @pl.when(step >= DEPTH)
        def _():
            tile_copy(tiles_ref, held, sems, step - DEPTH, True).wait()

        for j in range(UNROLL):
            word = list_ref[step * UNROLL + j]
            row, slot = row_of(word) & 63, slot_of(word)
            shift = jnp.left_shift(lax.shift_right_logical(word, jnp.int32(15)) * jnp.int32(HASH), 21)
            scaled = jnp.dot(near_ref[row], far[slot & 127], preferred_element_type=jnp.float32)
            mixed = pattern_ref[...] + shift
            mixed = mixed ^ jnp.left_shift(mixed, 5)
            tile = jnp.where(mixed < 0, pl.reciprocal(scaled, approx=True), 0.0).astype(jnp.bfloat16)
            held[buffer, j] = tile
            acc[slot] += jnp.dot(ex_ref[row], tile, preferred_element_type=jnp.float32)
        tile_copy(tiles_ref, held, sems, step, True).start()
        return carry

    lax.fori_loop(0, steps, turn, 0)
    encode(acc, out_ref)

    def drain(step, carry):
        tile_copy(tiles_ref, held, sems, step, True).wait()
        return carry

    lax.fori_loop(jnp.maximum(steps - DEPTH, 0), steps, drain, 0)


def stream(steps, tiles_ref, held, sems, use):
    def fetch(step, carry):
        tile_copy(tiles_ref, held, sems, step, False).start()
        return carry

    lax.fori_loop(0, jnp.minimum(steps, DEPTH - 1), fetch, 0)

    def turn(step, carry):
        @pl.when(step + DEPTH - 1 < steps)
        def _():
            fetch(step + DEPTH - 1, 0)

        tile_copy(tiles_ref, held, sems, step, False).wait()
        use(step, lax.rem(step, DEPTH))
        return carry

    lax.fori_loop(0, steps, turn, 0)


def columns_kernel(list_ref, steps_ref, tiles_ref, ex_ref, out_ref, acc, held, sems):
    acc[...] = jnp.zeros_like(acc)

    def use(step, buffer):
        for j in range(UNROLL):
            word = list_ref[step * UNROLL + j]
            row, slot = row_of(word) & 63, slot_of(word)
            acc[slot] += jnp.dot(ex_ref[row], held[buffer, j], preferred_element_type=jnp.float32)

    stream(steps_ref[0], tiles_ref, held, sems, use)
    encode(acc, out_ref)


def rows_kernel(list_ref, steps_ref, tiles_ref, ex_ref, out_ref, held, sems):
    out_ref[...] = jnp.zeros_like(out_ref)

    def use(step, buffer):
        for j in range(UNROLL):
            word = list_ref[step * UNROLL + j]
            row, slot = row_of(word), slot_of(word) & 127
            out_ref[row] += lax.dot_general(
                ex_ref[slot], held[buffer, j], (((1,), (1,)), ((), ())),
                preferred_element_type=jnp.float32,
            )

    stream(steps_ref[0], tiles_ref, held, sems, use)


HELD = pltpu.VMEM((DEPTH, UNROLL, BLOCK, BLOCK), jnp.bfloat16)
SEMS = pltpu.SemaphoreType.DMA((DEPTH,))


def build(pairs, steps, pattern, near, geometry, exitance, pair_max):
    slots, hours = geometry.shape[0], exitance.shape[1]
    return pl.pallas_call(
        build_kernel,
        in_specs=[SMEM_SPEC] * 2 + [VMEM_SPEC] * 4,
        out_specs=[ANY_SPEC, VMEM_SPEC],
        out_shape=[
            jax.ShapeDtypeStruct((pair_max, BLOCK, BLOCK), jnp.bfloat16),
            jax.ShapeDtypeStruct((slots, hours, BLOCK), jnp.int16),
        ],
        scratch_shapes=[
            pltpu.VMEM((slots + 1, hours, BLOCK), jnp.float32),
            HELD,
            SEMS,
            pltpu.VMEM((slots, FEATURES, BLOCK), jnp.bfloat16),
            pltpu.VMEM((8 * FEATURES, BLOCK), jnp.float32),
        ],
        compiler_params=pltpu.CompilerParams(vmem_limit_bytes=VMEM),
        cost_estimate=pl.CostEstimate(
            flops=20_000_000_000, bytes_accessed=60_000_000, transcendentals=10_000_000
        ),
    )(pairs, steps, pattern, near, geometry, exitance)


def columns(pairs, steps, tiles, exitance, slots):
    hours = exitance.shape[1]
    return pl.pallas_call(
        columns_kernel,
        in_specs=[SMEM_SPEC] * 2 + [ANY_SPEC, VMEM_SPEC],
        out_specs=VMEM_SPEC,
        out_shape=jax.ShapeDtypeStruct((slots, hours, BLOCK), jnp.int16),
        scratch_shapes=[pltpu.VMEM((slots + 1, hours, BLOCK), jnp.float32), HELD, SEMS],
        compiler_params=pltpu.CompilerParams(vmem_limit_bytes=VMEM),
        cost_estimate=pl.CostEstimate(flops=10_000_000_000, bytes_accessed=40_000_000, transcendentals=0),
    )(pairs, steps, tiles, exitance)


def rows(pairs, steps, tiles, fetched, row_blocks):
    hours = fetched.shape[1]
    return pl.pallas_call(
        rows_kernel,
        in_specs=[SMEM_SPEC] * 2 + [ANY_SPEC, VMEM_SPEC],
        out_specs=VMEM_SPEC,
        out_shape=jax.ShapeDtypeStruct((row_blocks + 1, hours, BLOCK), jnp.float32),
        scratch_shapes=[HELD, SEMS],
        compiler_params=pltpu.CompilerParams(vmem_limit_bytes=VMEM),
        cost_estimate=pl.CostEstimate(flops=10_000_000_000, bytes_accessed=40_000_000, transcendentals=0),
    )(pairs, steps, tiles, fetched)


def add_asked(acc, asked_ref, got_ref):
    def add(at, carry):
        acc[asked_ref[at, 0]] += decode(got_ref[at])
        return carry

    lax.fori_loop(0, got_ref.shape[0], add, 0, unroll=8)


def own_kernel(asked_ref, got_ref, out_ref):
    out_ref[...] = jnp.zeros_like(out_ref)
    add_asked(out_ref, asked_ref, got_ref)


def own(asked, got, blocks):
    return pl.pallas_call(
        own_kernel,
        in_specs=[SMEM_SPEC, VMEM_SPEC],
        out_specs=VMEM_SPEC,
        out_shape=jax.ShapeDtypeStruct((blocks,) + got.shape[1:], jnp.float32),
        compiler_params=pltpu.CompilerParams(vmem_limit_bytes=VMEM // 4),
        cost_estimate=pl.CostEstimate(flops=10_000_000, bytes_accessed=4_000_000, transcendentals=0),
    )(asked, got)


def middle_kernel(
    asked_ref, asked_other_ref, own_ref, got_ref, base_ref, albedo_ref, area_ref, ex_out_ref, send_ref,
    acc, ex, send, ex_sems, send_sems,
):
    acc[...] = own_ref[...]
    add_asked(acc, asked_other_ref, got_ref)
    ex[...] = (area_ref[...] * (base_ref[...] + albedo_ref[...] * acc[...])).astype(jnp.bfloat16)
    send_copies = part_copies(send, send_ref, send_sems)
    ex_copies = part_copies(ex, ex_out_ref, ex_sems)
    put_asked(asked_ref, ex, send, send_copies)
    for copy in ex_copies:
        copy.start()
    for copy in ex_copies + send_copies:
        copy.wait()


def middle(asked, asked_other, own_sum, got, base, albedo, area):
    blocks, hours, block = base.shape
    owners = asked.shape[0]
    return pl.pallas_call(
        middle_kernel,
        in_specs=[SMEM_SPEC] * 2 + [VMEM_SPEC] * 5,
        out_specs=[HBM_SPEC] * 2,
        out_shape=[
            jax.ShapeDtypeStruct((blocks, hours, block), jnp.bfloat16),
            jax.ShapeDtypeStruct((owners, hours, block), jnp.bfloat16),
        ],
        scratch_shapes=[
            pltpu.VMEM((blocks, hours, block), jnp.float32),
            pltpu.VMEM((blocks, hours, block), jnp.bfloat16),
            pltpu.VMEM((owners, hours, block), jnp.bfloat16),
            pltpu.SemaphoreType.DMA((PARTS,)),
            pltpu.SemaphoreType.DMA((PARTS,)),
        ],
        compiler_params=pltpu.CompilerParams(vmem_limit_bytes=VMEM // 4),
    )(asked, asked_other, own_sum, got, base, albedo, area)


def last_kernel(asked_other_ref, own_ref, got_ref, base_ref, albedo_ref, out_ref, acc, sems):
    acc[...] = own_ref[...]
    add_asked(acc, asked_other_ref, got_ref)
    size = acc.shape[0] // PARTS
    copies = part_copies(acc, out_ref, sems)
    for i, copy in enumerate(copies):
        part = slice(i * size, (i + 1) * size)
        acc[part] = base_ref[part] + albedo_ref[part] * acc[part]
        copy.start()
    for copy in copies:
        copy.wait()


def last(asked_other, own_sum, got, base, albedo):
    return pl.pallas_call(
        last_kernel,
        in_specs=[SMEM_SPEC] + [VMEM_SPEC] * 4,
        out_specs=HBM_SPEC,
        out_shape=jax.ShapeDtypeStruct(base.shape, jnp.float32),
        scratch_shapes=[
            pltpu.VMEM(base.shape, jnp.float32),
            pltpu.SemaphoreType.DMA((PARTS,)),
        ],
        compiler_params=pltpu.CompilerParams(vmem_limit_bytes=VMEM // 4),
    )(asked_other, own_sum, got, base, albedo)


def ask_kernel(core_ref, fetch_ref, out_ref):
    core = core_ref[0]
    for owner in range(out_ref.shape[0]):
        out_ref[owner] = jnp.full((1, BLOCK), fetch_ref[2 * owner + core], jnp.int32)


def ask(core, fetch_block, owners):
    return pl.pallas_call(
        ask_kernel,
        in_specs=[SMEM_SPEC] * 2,
        out_specs=VMEM_SPEC,
        out_shape=jax.ShapeDtypeStruct((owners, 1, BLOCK), jnp.int32),
    )(core.reshape(1), fetch_block)


def part_copies(source, target, sems):
    size = source.shape[0] // PARTS
    return [
        pltpu.make_async_copy(
            source.at[pl.ds(i * size, size)], target.at[pl.ds(i * size, size)], sems.at[i]
        )
        for i in range(PARTS)
    ]


def put_asked(asked_ref, ex_ref, send, copies):
    size = send.shape[0] // PARTS

    def put(at, carry):
        send[at] = ex_ref[asked_ref[at, 0]]
        return carry

    for i, copy in enumerate(copies):
        lax.fori_loop(i * size, (i + 1) * size, put, 0, unroll=8)
        copy.start()


def place_kernel(asked_ref, geometry_ref, place_ref, placed, sems):
    def put(at, carry):
        placed[at] = geometry_ref[pl.ds(asked_ref[at, 0], 1), :]
        return carry

    copies = part_copies(placed, place_ref, sems)
    size = placed.shape[0] // PARTS
    for i, copy in enumerate(copies):
        lax.fori_loop(i * size, (i + 1) * size, put, 0, unroll=8)
        copy.start()
    for copy in copies:
        copy.wait()


def place(asked, geometry):
    owners = asked.shape[0]
    return pl.pallas_call(
        place_kernel,
        in_specs=[SMEM_SPEC, VMEM_SPEC],
        out_specs=HBM_SPEC,
        out_shape=jax.ShapeDtypeStruct((owners, 1, geometry.shape[1]), jnp.float32),
        scratch_shapes=[
            pltpu.VMEM((owners, 1, geometry.shape[1]), jnp.float32),
            pltpu.SemaphoreType.DMA((PARTS,)),
        ],
        compiler_params=pltpu.CompilerParams(vmem_limit_bytes=VMEM // 4),
    )(asked, geometry)


def first_kernel(asked_ref, area_ref, emission_ref, ex_ref, send_ref, send, sems):
    ex_ref[...] = (area_ref[...] * emission_ref[...]).astype(jnp.bfloat16)
    copies = part_copies(send, send_ref, sems)
    put_asked(asked_ref, ex_ref, send, copies)
    for copy in copies:
        copy.wait()


def first(asked, area, emission):
    blocks, hours, block = emission.shape
    owners = asked.shape[0]
    return pl.pallas_call(
        first_kernel,
        in_specs=[SMEM_SPEC] + [VMEM_SPEC] * 2,
        out_specs=[VMEM_SPEC, HBM_SPEC],
        out_shape=[
            jax.ShapeDtypeStruct((blocks, hours, block), jnp.bfloat16),
            jax.ShapeDtypeStruct((owners, hours, block), jnp.bfloat16),
        ],
        scratch_shapes=[
            pltpu.VMEM((owners, hours, block), jnp.bfloat16),
            pltpu.SemaphoreType.DMA((PARTS,)),
        ],
        compiler_params=pltpu.CompilerParams(vmem_limit_bytes=VMEM // 4),
        cost_estimate=pl.CostEstimate(flops=10_000_000, bytes_accessed=8_000_000, transcendentals=0),
    )(asked, area, emission)


def factor_rows(x, y, z, area, facing, near):
    x, y, z = x - 3.0, y - 3.0, z - 3.0
    unit = (math.pi if near else 1.0) / facing
    norm = unit * (x * x + y * y + z * z + area)
    if near:
        terms = (norm, unit, -2.0 * unit * x, -2.0 * unit * y, -2.0 * unit * z)
        order = (0, 0, 1, 1, 0, 2)
    else:
        terms = (unit, norm, unit * x, unit * y, unit * z)
        order = (0, 1, 0, 1, 2, 0)
    found = []
    for term in terms:
        parts = []
        for _ in range(3):
            part = term.astype(jnp.bfloat16).astype(jnp.float32)
            parts.append(part)
            term = term - part
        found += [parts[i] for i in order]
    return found + [jnp.zeros_like(x)] * (FEATURES - len(found))


def factor_blocks(read, count, turned, near, put):
    def group(at, carry):
        for i, feature in enumerate(factor_rows(*read(pl.ds(pl.multiple_of(at * 8, 8), 8)), near)):
            turned[8 * i : 8 * i + 8, :] = feature
        for i in range(8):
            put(at * 8 + i, turned[pl.ds(i, FEATURES, stride=8), :])
        return carry

    lax.fori_loop(0, count // 8, group, 0)


def near_kernel(positions_ref, area_ref, facing_ref, out_ref, turned):
    def read(at):
        return [positions_ref[i, at, :] for i in range(3)] + [area_ref[at, :], facing_ref[at, :]]

    def put(at, block):
        out_ref[at] = block.T.astype(jnp.bfloat16)

    factor_blocks(read, out_ref.shape[0], turned, True, put)


def far_factors(geometry_ref, out, turned):
    def read(at):
        return [geometry_ref[at, 0, i * BLOCK : (i + 1) * BLOCK] for i in range(5)]

    def put(at, block):
        out[at] = block.astype(jnp.bfloat16)

    factor_blocks(read, out.shape[0], turned, False, put)


def factors(kernel, arrays, shape):
    return pl.pallas_call(
        kernel,
        in_specs=[VMEM_SPEC] * len(arrays),
        out_specs=VMEM_SPEC,
        out_shape=jax.ShapeDtypeStruct(shape, jnp.bfloat16),
        scratch_shapes=[pltpu.VMEM((8 * FEATURES, BLOCK), jnp.float32)],
        compiler_params=pltpu.CompilerParams(vmem_limit_bytes=VMEM),
        cost_estimate=pl.CostEstimate(flops=10_000_000, bytes_accessed=8_000_000, transcendentals=0),
    )(*arrays)


def local(
    emission, positions, patch_area, facing, albedo_class, albedo_table, fetch_block,
    pair_rows, pair_slots, pair_code,
):
    blocks, hours = emission.shape[:2]
    owners = lax.axis_size("blk")
    core = lax.axis_index("grp")

    def exchange(array):
        return lax.all_to_all(array, "blk", split_axis=0, concat_axis=0, tiled=True)

    def swap(array):
        return lax.ppermute(array, "grp", [(0, 1), (1, 0)])

    asked = exchange(ask(core, fetch_block, owners)).reshape(owners, BLOCK)

    def words(pair_row, pair_slot, code):
        skip = (pair_slot & 1) ^ core
        return pair_row | (skip << 6) | ((pair_slot >> 1) << 7) | jnp.left_shift(code, 15)

    lists = (pair_rows, pair_slots, pair_code)
    pairs, steps = pair_list(words(*lists), words(*map(swap, lists)))
    geometry = exchange(place(asked, jnp.concatenate([*positions, patch_area, facing], axis=1)))
    area = patch_area[:, None, :]
    near = factors(near_kernel, (positions, patch_area, facing), (blocks, BLOCK, FEATURES))
    exitance, send = first(asked, area, emission)
    asked_other = swap(asked)
    send, geometry, near, pairs, steps, asked_other = lax.optimization_barrier(
        (send, geometry, near, pairs, steps, asked_other)
    )

    class_ids = jnp.arange(NCLASS, dtype=jnp.int32)
    albedo = jnp.sum(
        jnp.where(albedo_class[..., None] == class_ids, albedo_table, jnp.float32(0.0)), axis=-1
    )[:, None, :]

    fetched = exchange(send)
    tiles, back = build(
        pairs, steps, jnp.asarray(hash_pattern()), near, geometry, exitance, 2 * pair_rows.shape[0]
    )

    def collect(back, fetched):
        got = exchange(back)
        to_rows = rows(pairs, steps, tiles, fetched, blocks)
        base = emission + albedo * (to_rows[:blocks] + swap(to_rows)[:blocks])
        got, base = lax.optimization_barrier((got, base))
        return own(asked, got, blocks), swap(got), base

    exitance, send = middle(asked, asked_other, *collect(back, fetched), albedo, area)
    fetched = exchange(send)
    back = columns(pairs, steps, tiles, exitance, owners)
    return last(asked_other, *collect(back, fetched), albedo)


def solution(mesh):
    in_specs = (
        P("blk", None, None),
        P(None, "blk", None),
        P("blk", None),
        P("blk", None),
        P("blk", None),
        P(),
        P("blk"),
        P(("blk", "grp")),
        P(("blk", "grp")),
        P(("blk", "grp")),
    )
    out_specs = P("blk", None, None)
    return jax.shard_map(local, mesh=mesh, in_specs=in_specs, out_specs=out_specs, check_vma=False)
```

```python
import math

import jax
import jax.numpy as jnp
import numpy as np
from jax import lax
from jax.experimental import pallas as pl
from jax.experimental.pallas import tpu as pltpu
from jax.sharding import PartitionSpec as P

BLOCK = 128
NCLASS = 8
HASH = 747796405
FEATURES = 32
UNROLL = 64
DEPTH = 4
VMEM = 60 * 1024 * 1024
SMEM_SPEC = pl.BlockSpec(memory_space=pltpu.SMEM)
VMEM_SPEC = pl.BlockSpec(memory_space=pltpu.VMEM)
ANY_SPEC = pl.BlockSpec(memory_space=pl.ANY)
HBM_SPEC = pl.BlockSpec(memory_space=pltpu.HBM)
PARTS = 4

SPARE = 64 | (128 << 7)


def hash_pattern():
    at = (np.arange(BLOCK * BLOCK, dtype=np.uint64) * HASH) & 0xFFFFFFFF
    odd = (at >> 2) ^ (at >> 6) ^ (at >> 7) ^ (at >> 11)
    word = (((at >> 14) << 21) + ((odd & 1) << 31)) & 0xFFFFFFFF
    return word.astype(np.uint32).astype(np.int32).reshape(BLOCK, BLOCK)


def row_of(word):
    return word & 127


def slot_of(word):
    return lax.shift_right_logical(word, jnp.int32(7)) & 255


def list_kernel(mine_ref, other_ref, asked_ref, list_ref, steps_ref, short_ref):
    for owner in range(asked_ref.shape[0]):
        short_ref[owner] = asked_ref[owner, 0]

    def take_from(words_ref):
        def take(turn, count):
            for j in range(8):
                word = words_ref[turn * 8 + j]
                list_ref[count] = word
                count = count + 1 - (lax.shift_right_logical(word, jnp.int32(6)) & 1)
            return count

        return take

    turns = mine_ref.shape[0] // 8
    count = lax.fori_loop(0, turns, take_from(mine_ref), jnp.int32(0))
    count = lax.fori_loop(0, turns, take_from(other_ref), count)
    for j in range(UNROLL):
        list_ref[count + j] = jnp.int32(SPARE)
    steps_ref[0] = jnp.maximum((count + UNROLL - 1) // UNROLL, 1)


def pair_list(mine, other, asked):
    return pl.pallas_call(
        list_kernel,
        out_shape=(
            jax.ShapeDtypeStruct((2 * mine.shape[0] + UNROLL,), jnp.int32),
            jax.ShapeDtypeStruct((1,), jnp.int32),
            jax.ShapeDtypeStruct((asked.shape[0],), jnp.int32),
        ),
        in_specs=[SMEM_SPEC] * 3,
        out_specs=(SMEM_SPEC,) * 3,
        cost_estimate=pl.CostEstimate(flops=10_000_000, bytes_accessed=10_000_000, transcendentals=0),
    )(mine, other, asked)


def encode(acc, out_ref):
    def one(slot, carry):
        value = acc[slot]
        top = jnp.max(value, axis=0, keepdims=True)
        exponent = jnp.ceil(jnp.log2(jnp.maximum(top, 1e-30)))
        level = jnp.minimum(jnp.round(value * jnp.exp2(15.0 - exponent)), 32767.0).astype(jnp.int32)
        biased = exponent.astype(jnp.int32) + 128
        places = lax.broadcasted_iota(jnp.int32, value.shape, 0)
        mark = jnp.where(places < 8, lax.shift_right_logical(biased, jnp.minimum(places, 8)) & 1, 0)
        out_ref[slot] = (level ^ -mark).astype(jnp.int16)
        return carry

    lax.fori_loop(0, out_ref.shape[0], one, 0, unroll=4)


def decode(code):
    code = code.astype(jnp.int32)
    head = code[:8]
    places = lax.broadcasted_iota(jnp.int32, head.shape, 0)
    bits = jnp.where(head < 0, jnp.left_shift(jnp.ones_like(head), places), 0).astype(jnp.float32)
    biased = jnp.sum(bits, axis=0, keepdims=True)
    level = code ^ lax.shift_right_arithmetic(code, jnp.full_like(code, 31))
    return level.astype(jnp.float32) * jnp.exp2(biased - (128.0 + 15.0))


def tile_copy(tiles_ref, held, sems, step, out):
    buffer = lax.rem(step, DEPTH)
    away = tiles_ref.at[pl.ds(step * UNROLL, UNROLL)]
    here = held.at[buffer]
    source, target = (here, away) if out else (away, here)
    return pltpu.make_async_copy(source, target, sems.at[buffer])


def build_kernel(
    list_ref, steps_ref, pattern_ref, near_ref, geometry_ref, ex_ref, tiles_ref, out_ref,
    acc, held, sems, far, turned,
):
    steps = steps_ref[0]
    far_factors(geometry_ref, far, turned)
    acc[...] = jnp.zeros_like(acc)

    def turn(step, carry):
        buffer = lax.rem(step, DEPTH)

        @pl.when(step >= DEPTH)
        def _():
            tile_copy(tiles_ref, held, sems, step - DEPTH, True).wait()

        for j in range(UNROLL):
            word = list_ref[step * UNROLL + j]
            row, slot = row_of(word) & 63, slot_of(word)
            shift = jnp.left_shift(lax.shift_right_logical(word, jnp.int32(15)) * jnp.int32(HASH), 21)
            scaled = jnp.dot(near_ref[row], far[slot & 127], preferred_element_type=jnp.float32)
            mixed = pattern_ref[...] + shift
            mixed = mixed ^ jnp.left_shift(mixed, 5)
            tile = jnp.where(mixed < 0, pl.reciprocal(scaled, approx=True), 0.0).astype(jnp.bfloat16)
            held[buffer, j] = tile
            acc[slot] += jnp.dot(ex_ref[row], tile, preferred_element_type=jnp.float32)
        tile_copy(tiles_ref, held, sems, step, True).start()
        return carry

    lax.fori_loop(0, steps, turn, 0)
    encode(acc, out_ref)

    def drain(step, carry):
        tile_copy(tiles_ref, held, sems, step, True).wait()
        return carry

    lax.fori_loop(jnp.maximum(steps - DEPTH, 0), steps, drain, 0)


def stream(steps, tiles_ref, held, sems, use):
    def fetch(step, carry):
        tile_copy(tiles_ref, held, sems, step, False).start()
        return carry

    lax.fori_loop(0, jnp.minimum(steps, DEPTH - 1), fetch, 0)

    def turn(step, carry):
        @pl.when(step + DEPTH - 1 < steps)
        def _():
            fetch(step + DEPTH - 1, 0)

        tile_copy(tiles_ref, held, sems, step, False).wait()
        use(step, lax.rem(step, DEPTH))
        return carry

    lax.fori_loop(0, steps, turn, 0)


def columns_kernel(list_ref, steps_ref, tiles_ref, ex_ref, out_ref, acc, held, sems):
    acc[...] = jnp.zeros_like(acc)

    def use(step, buffer):
        for j in range(UNROLL):
            word = list_ref[step * UNROLL + j]
            row, slot = row_of(word) & 63, slot_of(word)
            acc[slot] += jnp.dot(ex_ref[row], held[buffer, j], preferred_element_type=jnp.float32)

    stream(steps_ref[0], tiles_ref, held, sems, use)
    encode(acc, out_ref)


def rows_kernel(list_ref, steps_ref, tiles_ref, ex_ref, out_ref, held, sems):
    out_ref[...] = jnp.zeros_like(out_ref)

    def use(step, buffer):
        for j in range(UNROLL):
            word = list_ref[step * UNROLL + j]
            row, slot = row_of(word), slot_of(word) & 127
            out_ref[row] += lax.dot_general(
                ex_ref[slot], held[buffer, j], (((1,), (1,)), ((), ())),
                preferred_element_type=jnp.float32,
            )

    stream(steps_ref[0], tiles_ref, held, sems, use)


HELD = pltpu.VMEM((DEPTH, UNROLL, BLOCK, BLOCK), jnp.bfloat16)
SEMS = pltpu.SemaphoreType.DMA((DEPTH,))


def build(pairs, steps, pattern, near, geometry, exitance, pair_max):
    slots, hours = geometry.shape[0], exitance.shape[1]
    return pl.pallas_call(
        build_kernel,
        in_specs=[SMEM_SPEC] * 2 + [VMEM_SPEC] * 4,
        out_specs=[ANY_SPEC, VMEM_SPEC],
        out_shape=[
            jax.ShapeDtypeStruct((pair_max, BLOCK, BLOCK), jnp.bfloat16),
            jax.ShapeDtypeStruct((slots, hours, BLOCK), jnp.int16),
        ],
        scratch_shapes=[
            pltpu.VMEM((slots + 1, hours, BLOCK), jnp.float32),
            HELD,
            SEMS,
            pltpu.VMEM((slots, FEATURES, BLOCK), jnp.bfloat16),
            pltpu.VMEM((8 * FEATURES, BLOCK), jnp.float32),
        ],
        compiler_params=pltpu.CompilerParams(vmem_limit_bytes=VMEM),
        cost_estimate=pl.CostEstimate(
            flops=20_000_000_000, bytes_accessed=60_000_000, transcendentals=10_000_000
        ),
    )(pairs, steps, pattern, near, geometry, exitance)


def columns(pairs, steps, tiles, exitance, slots):
    hours = exitance.shape[1]
    return pl.pallas_call(
        columns_kernel,
        in_specs=[SMEM_SPEC] * 2 + [ANY_SPEC, VMEM_SPEC],
        out_specs=VMEM_SPEC,
        out_shape=jax.ShapeDtypeStruct((slots, hours, BLOCK), jnp.int16),
        scratch_shapes=[pltpu.VMEM((slots + 1, hours, BLOCK), jnp.float32), HELD, SEMS],
        compiler_params=pltpu.CompilerParams(vmem_limit_bytes=VMEM),
        cost_estimate=pl.CostEstimate(flops=10_000_000_000, bytes_accessed=40_000_000, transcendentals=0),
    )(pairs, steps, tiles, exitance)


def rows(pairs, steps, tiles, fetched, row_blocks):
    hours = fetched.shape[1]
    return pl.pallas_call(
        rows_kernel,
        in_specs=[SMEM_SPEC] * 2 + [ANY_SPEC, VMEM_SPEC],
        out_specs=VMEM_SPEC,
        out_shape=jax.ShapeDtypeStruct((row_blocks + 1, hours, BLOCK), jnp.float32),
        scratch_shapes=[HELD, SEMS],
        compiler_params=pltpu.CompilerParams(vmem_limit_bytes=VMEM),
        cost_estimate=pl.CostEstimate(flops=10_000_000_000, bytes_accessed=40_000_000, transcendentals=0),
    )(pairs, steps, tiles, fetched)


def add_asked(acc, asked_ref, got_ref):
    def add(at, carry):
        acc[asked_ref[at]] += decode(got_ref[at])
        return carry

    lax.fori_loop(0, got_ref.shape[0], add, 0, unroll=8)


def own_kernel(asked_ref, got_ref, out_ref):
    out_ref[...] = jnp.zeros_like(out_ref)
    add_asked(out_ref, asked_ref, got_ref)


def own(asked, got, blocks):
    return pl.pallas_call(
        own_kernel,
        in_specs=[SMEM_SPEC, VMEM_SPEC],
        out_specs=VMEM_SPEC,
        out_shape=jax.ShapeDtypeStruct((blocks,) + got.shape[1:], jnp.float32),
        compiler_params=pltpu.CompilerParams(vmem_limit_bytes=VMEM // 4),
        cost_estimate=pl.CostEstimate(flops=10_000_000, bytes_accessed=4_000_000, transcendentals=0),
    )(asked, got)


def middle_kernel(
    asked_ref, asked_other_ref, own_ref, got_ref, base_ref, albedo_ref, area_ref, ex_out_ref, send_ref,
    acc, ex, send, ex_sems, send_sems,
):
    acc[...] = own_ref[...]
    add_asked(acc, asked_other_ref, got_ref)
    ex[...] = (area_ref[...] * (base_ref[...] + albedo_ref[...] * acc[...])).astype(jnp.bfloat16)
    send_copies = part_copies(send, send_ref, send_sems)
    ex_copies = part_copies(ex, ex_out_ref, ex_sems)
    put_asked(asked_ref, ex, send, send_copies)
    for copy in ex_copies:
        copy.start()
    for copy in ex_copies + send_copies:
        copy.wait()


def middle(asked, asked_other, own_sum, got, base, albedo, area):
    blocks, hours, block = base.shape
    owners = asked.shape[0]
    return pl.pallas_call(
        middle_kernel,
        in_specs=[SMEM_SPEC] * 2 + [VMEM_SPEC] * 5,
        out_specs=[HBM_SPEC] * 2,
        out_shape=[
            pltpu.HBM((blocks, hours, block), jnp.bfloat16),
            pltpu.HBM((owners, hours, block), jnp.bfloat16),
        ],
        scratch_shapes=[
            pltpu.VMEM((blocks, hours, block), jnp.float32),
            pltpu.VMEM((blocks, hours, block), jnp.bfloat16),
            pltpu.VMEM((owners, hours, block), jnp.bfloat16),
            pltpu.SemaphoreType.DMA((PARTS,)),
            pltpu.SemaphoreType.DMA((PARTS,)),
        ],
        compiler_params=pltpu.CompilerParams(vmem_limit_bytes=VMEM // 4),
    )(asked, asked_other, own_sum, got, base, albedo, area)


def last_kernel(asked_other_ref, own_ref, got_ref, base_ref, albedo_ref, out_ref, acc, sems):
    acc[...] = own_ref[...]
    add_asked(acc, asked_other_ref, got_ref)
    size = acc.shape[0] // PARTS
    copies = part_copies(acc, out_ref, sems)
    for i, copy in enumerate(copies):
        part = slice(i * size, (i + 1) * size)
        acc[part] = base_ref[part] + albedo_ref[part] * acc[part]
        copy.start()
    for copy in copies:
        copy.wait()


def last(asked_other, own_sum, got, base, albedo):
    return pl.pallas_call(
        last_kernel,
        in_specs=[SMEM_SPEC] + [VMEM_SPEC] * 4,
        out_specs=HBM_SPEC,
        out_shape=jax.ShapeDtypeStruct(base.shape, jnp.float32),
        scratch_shapes=[
            pltpu.VMEM(base.shape, jnp.float32),
            pltpu.SemaphoreType.DMA((PARTS,)),
        ],
        compiler_params=pltpu.CompilerParams(vmem_limit_bytes=VMEM // 4),
    )(asked_other, own_sum, got, base, albedo)


def ask_kernel(core_ref, fetch_ref, out_ref):
    core = core_ref[0]
    for owner in range(out_ref.shape[0]):
        out_ref[owner] = jnp.full((1, BLOCK), fetch_ref[2 * owner + core], jnp.int32)


def ask(core, fetch_block, owners):
    return pl.pallas_call(
        ask_kernel,
        in_specs=[SMEM_SPEC] * 2,
        out_specs=VMEM_SPEC,
        out_shape=jax.ShapeDtypeStruct((owners, 1, BLOCK), jnp.int32),
    )(core.reshape(1), fetch_block)


def part_copies(source, target, sems):
    size = source.shape[0] // PARTS
    return [
        pltpu.make_async_copy(
            source.at[pl.ds(i * size, size)], target.at[pl.ds(i * size, size)], sems.at[i]
        )
        for i in range(PARTS)
    ]


def put_asked(asked_ref, ex_ref, send, copies):
    size = send.shape[0] // PARTS

    def put(at, carry):
        send[at] = ex_ref[asked_ref[at]]
        return carry

    for i, copy in enumerate(copies):
        lax.fori_loop(i * size, (i + 1) * size, put, 0, unroll=8)
        copy.start()


def place_kernel(asked_ref, geometry_ref, place_ref, placed, sems):
    def put(at, carry):
        placed[at] = geometry_ref[pl.ds(asked_ref[at, 0], 1), :]
        return carry

    copies = part_copies(placed, place_ref, sems)
    size = placed.shape[0] // PARTS
    for i, copy in enumerate(copies):
        lax.fori_loop(i * size, (i + 1) * size, put, 0, unroll=8)
        copy.start()
    for copy in copies:
        copy.wait()


def place(asked, geometry):
    owners = asked.shape[0]
    return pl.pallas_call(
        place_kernel,
        in_specs=[SMEM_SPEC, VMEM_SPEC],
        out_specs=HBM_SPEC,
        out_shape=jax.ShapeDtypeStruct((owners, 1, geometry.shape[1]), jnp.float32),
        scratch_shapes=[
            pltpu.VMEM((owners, 1, geometry.shape[1]), jnp.float32),
            pltpu.SemaphoreType.DMA((PARTS,)),
        ],
        compiler_params=pltpu.CompilerParams(vmem_limit_bytes=VMEM // 4),
    )(asked, geometry)


def first_kernel(asked_ref, area_ref, emission_ref, ex_out_ref, send_ref, ex, send, ex_sems, send_sems):
    ex[...] = (area_ref[...] * emission_ref[...]).astype(jnp.bfloat16)
    ex_copies = part_copies(ex, ex_out_ref, ex_sems)
    send_copies = part_copies(send, send_ref, send_sems)
    put_asked(asked_ref, ex, send, send_copies)
    for copy in ex_copies:
        copy.start()
    for copy in ex_copies + send_copies:
        copy.wait()


def first(asked, area, emission):
    blocks, hours, block = emission.shape
    owners = asked.shape[0]
    return pl.pallas_call(
        first_kernel,
        in_specs=[SMEM_SPEC] + [VMEM_SPEC] * 2,
        out_specs=[HBM_SPEC] * 2,
        out_shape=[
            pltpu.HBM((blocks, hours, block), jnp.bfloat16),
            pltpu.HBM((owners, hours, block), jnp.bfloat16),
        ],
        scratch_shapes=[
            pltpu.VMEM((blocks, hours, block), jnp.bfloat16),
            pltpu.VMEM((owners, hours, block), jnp.bfloat16),
            pltpu.SemaphoreType.DMA((PARTS,)),
            pltpu.SemaphoreType.DMA((PARTS,)),
        ],
        compiler_params=pltpu.CompilerParams(vmem_limit_bytes=VMEM // 4),
        cost_estimate=pl.CostEstimate(flops=10_000_000, bytes_accessed=8_000_000, transcendentals=0),
    )(asked, area, emission)


def factor_rows(x, y, z, area, facing, near):
    x, y, z = x - 3.0, y - 3.0, z - 3.0
    unit = (math.pi if near else 1.0) / facing
    norm = unit * (x * x + y * y + z * z + area)
    if near:
        terms = (norm, unit, -2.0 * unit * x, -2.0 * unit * y, -2.0 * unit * z)
        order = (0, 0, 1, 1, 0, 2)
    else:
        terms = (unit, norm, unit * x, unit * y, unit * z)
        order = (0, 1, 0, 1, 2, 0)
    found = []
    for term in terms:
        parts = []
        for _ in range(3):
            part = term.astype(jnp.bfloat16).astype(jnp.float32)
            parts.append(part)
            term = term - part
        found += [parts[i] for i in order]
    return found + [jnp.zeros_like(x)] * (FEATURES - len(found))


def factor_blocks(read, count, turned, near, put):
    def group(at, carry):
        for i, feature in enumerate(factor_rows(*read(pl.ds(pl.multiple_of(at * 8, 8), 8)), near)):
            turned[8 * i : 8 * i + 8, :] = feature
        for i in range(8):
            put(at * 8 + i, turned[pl.ds(i, FEATURES, stride=8), :])
        return carry

    lax.fori_loop(0, count // 8, group, 0)


def near_kernel(positions_ref, area_ref, facing_ref, out_ref, geometry_ref, turned):
    parts = [positions_ref[i] for i in range(3)] + [area_ref[...], facing_ref[...]]
    for i, part in enumerate(parts):
        geometry_ref[:, i * BLOCK : (i + 1) * BLOCK] = part

    def read(at):
        return [positions_ref[i, at, :] for i in range(3)] + [area_ref[at, :], facing_ref[at, :]]

    def put(at, block):
        out_ref[at] = block.T.astype(jnp.bfloat16)

    factor_blocks(read, out_ref.shape[0], turned, True, put)


def far_factors(geometry_ref, out, turned):
    def read(at):
        return [geometry_ref[at, 0, i * BLOCK : (i + 1) * BLOCK] for i in range(5)]

    def put(at, block):
        out[at] = block.astype(jnp.bfloat16)

    factor_blocks(read, out.shape[0], turned, False, put)


def near_factors(positions, patch_area, facing):
    blocks = patch_area.shape[0]
    return pl.pallas_call(
        near_kernel,
        in_specs=[VMEM_SPEC] * 3,
        out_specs=[VMEM_SPEC] * 2,
        out_shape=[
            jax.ShapeDtypeStruct((blocks, BLOCK, FEATURES), jnp.bfloat16),
            jax.ShapeDtypeStruct((blocks, 5 * BLOCK), jnp.float32),
        ],
        scratch_shapes=[pltpu.VMEM((8 * FEATURES, BLOCK), jnp.float32)],
        compiler_params=pltpu.CompilerParams(vmem_limit_bytes=VMEM // 4),
        cost_estimate=pl.CostEstimate(flops=10_000_000, bytes_accessed=8_000_000, transcendentals=0),
    )(positions, patch_area, facing)


def local(
    emission, positions, patch_area, facing, albedo_class, albedo_table, fetch_block,
    pair_rows, pair_slots, pair_code,
):
    blocks, hours = emission.shape[:2]
    owners = lax.axis_size("blk")
    core = lax.axis_index("grp")

    def exchange(array):
        return lax.all_to_all(array, "blk", split_axis=0, concat_axis=0, tiled=True)

    def swap(array):
        return lax.ppermute(array, "grp", [(0, 1), (1, 0)])

    asked_rows = exchange(ask(core, fetch_block, owners)).reshape(owners, BLOCK)
    near, own_geometry = near_factors(positions, patch_area, facing)
    geometry = exchange(place(asked_rows, own_geometry))

    def words(pair_row, pair_slot, code):
        skip = (pair_slot & 1) ^ core
        return pair_row | (skip << 6) | ((pair_slot >> 1) << 7) | jnp.left_shift(code, 15)

    lists = (pair_rows, pair_slots, pair_code)
    pairs, steps, asked = pair_list(words(*lists), words(*map(swap, lists)), asked_rows)
    asked_other = swap(asked)
    area = patch_area[:, None, :]
    exitance, send = first(asked, area, emission)
    send, geometry, near, pairs, steps, asked_other = lax.optimization_barrier(
        (send, geometry, near, pairs, steps, asked_other)
    )

    class_ids = jnp.arange(NCLASS, dtype=jnp.int32)
    albedo = jnp.sum(
        jnp.where(albedo_class[..., None] == class_ids, albedo_table, jnp.float32(0.0)), axis=-1
    )[:, None, :]

    fetched = exchange(send)
    tiles, back = build(
        pairs, steps, jnp.asarray(hash_pattern()), near, geometry, exitance, 2 * pair_rows.shape[0]
    )

    def collect(back, fetched):
        got = exchange(back)
        to_rows = rows(pairs, steps, tiles, fetched, blocks)
        base = emission + albedo * (to_rows[:blocks] + swap(to_rows)[:blocks])
        got, base = lax.optimization_barrier((got, base))
        return own(asked, got, blocks), swap(got), base

    exitance, send = middle(asked, asked_other, *collect(back, fetched), albedo, area)
    fetched = exchange(send)
    back = columns(pairs, steps, tiles, exitance, owners)
    return last(asked_other, *collect(back, fetched), albedo)


def solution(mesh):
    in_specs = (
        P("blk", None, None),
        P(None, "blk", None),
        P("blk", None),
        P("blk", None),
        P("blk", None),
        P(),
        P("blk"),
        P(("blk", "grp")),
        P(("blk", "grp")),
        P(("blk", "grp")),
    )
    out_specs = P("blk", None, None)
    return jax.shard_map(local, mesh=mesh, in_specs=in_specs, out_specs=out_specs, check_vma=False)
```

```python
import math

import jax
import jax.numpy as jnp
import numpy as np
from jax import lax
from jax.experimental import pallas as pl
from jax.experimental.pallas import tpu as pltpu
from jax.sharding import PartitionSpec as P

BLOCK = 128
NCLASS = 8
HASH = 747796405
FEATURES = 32
UNROLL = 64
DEPTH = 4
VMEM = 60 * 1024 * 1024
SMEM_SPEC = pl.BlockSpec(memory_space=pltpu.SMEM)
VMEM_SPEC = pl.BlockSpec(memory_space=pltpu.VMEM)
ANY_SPEC = pl.BlockSpec(memory_space=pl.ANY)
HBM_SPEC = pl.BlockSpec(memory_space=pltpu.HBM)
PARTS = 4

SPARE = 64 | (128 << 7)


def hash_pattern():
    at = (np.arange(BLOCK * BLOCK, dtype=np.uint64) * HASH) & 0xFFFFFFFF
    odd = (at >> 2) ^ (at >> 6) ^ (at >> 7) ^ (at >> 11)
    word = (((at >> 14) << 21) + ((odd & 1) << 31)) & 0xFFFFFFFF
    return word.astype(np.uint32).astype(np.int32).reshape(BLOCK, BLOCK)


def row_of(word):
    return word & 127


def slot_of(word):
    return lax.shift_right_logical(word, jnp.int32(7)) & 255


def list_kernel(mine_ref, other_ref, list_ref, steps_ref):
    def take_from(words_ref):
        def take(turn, count):
            for j in range(8):
                word = words_ref[turn * 8 + j]
                list_ref[count] = word
                count = count + 1 - (lax.shift_right_logical(word, jnp.int32(6)) & 1)
            return count

        return take

    turns = mine_ref.shape[0] // 8
    count = lax.fori_loop(0, turns, take_from(mine_ref), jnp.int32(0))
    count = lax.fori_loop(0, turns, take_from(other_ref), count)
    for j in range(UNROLL):
        list_ref[count + j] = jnp.int32(SPARE)
    steps_ref[0] = jnp.maximum((count + UNROLL - 1) // UNROLL, 1)


def pair_list(mine, other):
    return pl.pallas_call(
        list_kernel,
        out_shape=(
            jax.ShapeDtypeStruct((2 * mine.shape[0] + UNROLL,), jnp.int32),
            jax.ShapeDtypeStruct((1,), jnp.int32),
        ),
        in_specs=[SMEM_SPEC] * 2,
        out_specs=(SMEM_SPEC,) * 2,
        cost_estimate=pl.CostEstimate(flops=10_000_000, bytes_accessed=10_000_000, transcendentals=0),
    )(mine, other)


def encode(acc, out_ref):
    def one(slot, carry):
        value = acc[slot]
        top = jnp.max(value, axis=0, keepdims=True)
        exponent = jnp.ceil(jnp.log2(jnp.maximum(top, 1e-30)))
        level = jnp.minimum(jnp.round(value * jnp.exp2(15.0 - exponent)), 32767.0).astype(jnp.int32)
        biased = exponent.astype(jnp.int32) + 128
        places = lax.broadcasted_iota(jnp.int32, value.shape, 0)
        mark = jnp.where(places < 8, lax.shift_right_logical(biased, jnp.minimum(places, 8)) & 1, 0)
        out_ref[slot] = (level ^ -mark).astype(jnp.int16)
        return carry

    lax.fori_loop(0, out_ref.shape[0], one, 0, unroll=4)


def decode(code):
    code = code.astype(jnp.int32)
    head = code[:8]
    places = lax.broadcasted_iota(jnp.int32, head.shape, 0)
    bits = jnp.where(head < 0, jnp.left_shift(jnp.ones_like(head), places), 0).astype(jnp.float32)
    biased = jnp.sum(bits, axis=0, keepdims=True)
    level = code ^ lax.shift_right_arithmetic(code, jnp.full_like(code, 31))
    return level.astype(jnp.float32) * jnp.exp2(biased - (128.0 + 15.0))


def tile_copy(tiles_ref, held, sems, step, out):
    buffer = lax.rem(step, DEPTH)
    away = tiles_ref.at[pl.ds(step * UNROLL, UNROLL)]
    here = held.at[buffer]
    source, target = (here, away) if out else (away, here)
    return pltpu.make_async_copy(source, target, sems.at[buffer])


def build_kernel(
    list_ref, steps_ref, pattern_ref, near_ref, geometry_ref, ex_ref, tiles_ref, out_ref,
    acc, held, sems, far, turned,
):
    steps = steps_ref[0]
    far_factors(geometry_ref, far, turned)
    acc[...] = jnp.zeros_like(acc)

    def turn(step, carry):
        buffer = lax.rem(step, DEPTH)

        @pl.when(step >= DEPTH)
        def _():
            tile_copy(tiles_ref, held, sems, step - DEPTH, True).wait()

        for j in range(UNROLL):
            word = list_ref[step * UNROLL + j]
            row, slot = row_of(word) & 63, slot_of(word)
            shift = jnp.left_shift(lax.shift_right_logical(word, jnp.int32(15)) * jnp.int32(HASH), 21)
            scaled = jnp.dot(near_ref[row], far[slot & 127], preferred_element_type=jnp.float32)
            mixed = pattern_ref[...] + shift
            mixed = mixed ^ jnp.left_shift(mixed, 5)
            tile = jnp.where(mixed < 0, pl.reciprocal(scaled, approx=True), 0.0).astype(jnp.bfloat16)
            held[buffer, j] = tile
            acc[slot] += jnp.dot(ex_ref[row], tile, preferred_element_type=jnp.float32)
        tile_copy(tiles_ref, held, sems, step, True).start()
        return carry

    lax.fori_loop(0, steps, turn, 0)
    encode(acc, out_ref)

    def drain(step, carry):
        tile_copy(tiles_ref, held, sems, step, True).wait()
        return carry

    lax.fori_loop(jnp.maximum(steps - DEPTH, 0), steps, drain, 0)


def stream(steps, tiles_ref, held, sems, use):
    def fetch(step, carry):
        tile_copy(tiles_ref, held, sems, step, False).start()
        return carry

    lax.fori_loop(0, jnp.minimum(steps, DEPTH - 1), fetch, 0)

    def turn(step, carry):
        @pl.when(step + DEPTH - 1 < steps)
        def _():
            fetch(step + DEPTH - 1, 0)

        tile_copy(tiles_ref, held, sems, step, False).wait()
        use(step, lax.rem(step, DEPTH))
        return carry

    lax.fori_loop(0, steps, turn, 0)


def columns_kernel(list_ref, steps_ref, tiles_ref, ex_ref, out_ref, acc, held, sems):
    acc[...] = jnp.zeros_like(acc)

    def use(step, buffer):
        for j in range(UNROLL):
            word = list_ref[step * UNROLL + j]
            row, slot = row_of(word) & 63, slot_of(word)
            acc[slot] += jnp.dot(ex_ref[row], held[buffer, j], preferred_element_type=jnp.float32)

    stream(steps_ref[0], tiles_ref, held, sems, use)
    encode(acc, out_ref)


def rows_kernel(list_ref, steps_ref, tiles_ref, ex_ref, out_ref, held, sems):
    out_ref[...] = jnp.zeros_like(out_ref)

    def use(step, buffer):
        for j in range(UNROLL):
            word = list_ref[step * UNROLL + j]
            row, slot = row_of(word), slot_of(word) & 127
            out_ref[row] += lax.dot_general(
                ex_ref[slot], held[buffer, j], (((1,), (1,)), ((), ())),
                preferred_element_type=jnp.float32,
            )

    stream(steps_ref[0], tiles_ref, held, sems, use)


HELD = pltpu.VMEM((DEPTH, UNROLL, BLOCK, BLOCK), jnp.bfloat16)
SEMS = pltpu.SemaphoreType.DMA((DEPTH,))


def build(pairs, steps, pattern, near, geometry, exitance, pair_max):
    slots, hours = geometry.shape[0], exitance.shape[1]
    return pl.pallas_call(
        build_kernel,
        in_specs=[SMEM_SPEC] * 2 + [VMEM_SPEC] * 4,
        out_specs=[ANY_SPEC, VMEM_SPEC],
        out_shape=[
            jax.ShapeDtypeStruct((pair_max, BLOCK, BLOCK), jnp.bfloat16),
            jax.ShapeDtypeStruct((slots, hours, BLOCK), jnp.int16),
        ],
        scratch_shapes=[
            pltpu.VMEM((slots + 1, hours, BLOCK), jnp.float32),
            HELD,
            SEMS,
            pltpu.VMEM((slots, FEATURES, BLOCK), jnp.bfloat16),
            pltpu.VMEM((8 * FEATURES, BLOCK), jnp.float32),
        ],
        compiler_params=pltpu.CompilerParams(vmem_limit_bytes=VMEM),
        cost_estimate=pl.CostEstimate(
            flops=20_000_000_000, bytes_accessed=60_000_000, transcendentals=10_000_000
        ),
    )(pairs, steps, pattern, near, geometry, exitance)


def columns(pairs, steps, tiles, exitance, slots):
    hours = exitance.shape[1]
    return pl.pallas_call(
        columns_kernel,
        in_specs=[SMEM_SPEC] * 2 + [ANY_SPEC, VMEM_SPEC],
        out_specs=VMEM_SPEC,
        out_shape=jax.ShapeDtypeStruct((slots, hours, BLOCK), jnp.int16),
        scratch_shapes=[pltpu.VMEM((slots + 1, hours, BLOCK), jnp.float32), HELD, SEMS],
        compiler_params=pltpu.CompilerParams(vmem_limit_bytes=VMEM),
        cost_estimate=pl.CostEstimate(flops=10_000_000_000, bytes_accessed=40_000_000, transcendentals=0),
    )(pairs, steps, tiles, exitance)


def rows(pairs, steps, tiles, fetched, row_blocks):
    hours = fetched.shape[1]
    return pl.pallas_call(
        rows_kernel,
        in_specs=[SMEM_SPEC] * 2 + [ANY_SPEC, VMEM_SPEC],
        out_specs=VMEM_SPEC,
        out_shape=jax.ShapeDtypeStruct((row_blocks + 1, hours, BLOCK), jnp.float32),
        scratch_shapes=[HELD, SEMS],
        compiler_params=pltpu.CompilerParams(vmem_limit_bytes=VMEM),
        cost_estimate=pl.CostEstimate(flops=10_000_000_000, bytes_accessed=40_000_000, transcendentals=0),
    )(pairs, steps, tiles, fetched)


def add_asked(acc, asked_ref, got_ref):
    def add(at, carry):
        acc[asked_ref[at]] += decode(got_ref[at])
        return carry

    lax.fori_loop(0, got_ref.shape[0], add, 0, unroll=8)


def own_kernel(asked_ref, got_ref, out_ref):
    out_ref[...] = jnp.zeros_like(out_ref)
    add_asked(out_ref, asked_ref, got_ref)


def own(asked, got, blocks):
    return pl.pallas_call(
        own_kernel,
        in_specs=[SMEM_SPEC, VMEM_SPEC],
        out_specs=VMEM_SPEC,
        out_shape=jax.ShapeDtypeStruct((blocks,) + got.shape[1:], jnp.float32),
        compiler_params=pltpu.CompilerParams(vmem_limit_bytes=VMEM // 4),
        cost_estimate=pl.CostEstimate(flops=10_000_000, bytes_accessed=4_000_000, transcendentals=0),
    )(asked, got)


def middle_kernel(
    asked_ref, asked_other_ref, own_ref, got_ref, base_ref, albedo_ref, area_ref, ex_out_ref, send_ref,
    acc, ex, send, ex_sems, send_sems,
):
    acc[...] = own_ref[...]
    add_asked(acc, asked_other_ref, got_ref)
    ex[...] = (area_ref[...] * (base_ref[...] + albedo_ref[...] * acc[...])).astype(jnp.bfloat16)
    send_copies = part_copies(send, send_ref, send_sems)
    ex_copies = part_copies(ex, ex_out_ref, ex_sems)
    put_asked(asked_ref, ex, send, send_copies)
    for copy in ex_copies:
        copy.start()
    for copy in ex_copies + send_copies:
        copy.wait()


def middle(asked, asked_other, own_sum, got, base, albedo, area):
    blocks, hours, block = base.shape
    owners = asked.shape[0]
    return pl.pallas_call(
        middle_kernel,
        in_specs=[SMEM_SPEC] * 2 + [VMEM_SPEC] * 5,
        out_specs=[HBM_SPEC] * 2,
        out_shape=[
            pltpu.HBM((blocks, hours, block), jnp.bfloat16),
            pltpu.HBM((owners, hours, block), jnp.bfloat16),
        ],
        scratch_shapes=[
            pltpu.VMEM((blocks, hours, block), jnp.float32),
            pltpu.VMEM((blocks, hours, block), jnp.bfloat16),
            pltpu.VMEM((owners, hours, block), jnp.bfloat16),
            pltpu.SemaphoreType.DMA((PARTS,)),
            pltpu.SemaphoreType.DMA((PARTS,)),
        ],
        compiler_params=pltpu.CompilerParams(vmem_limit_bytes=VMEM // 4),
    )(asked, asked_other, own_sum, got, base, albedo, area)


def last_kernel(asked_other_ref, own_ref, got_ref, base_ref, albedo_ref, out_ref, acc, sems):
    acc[...] = own_ref[...]
    add_asked(acc, asked_other_ref, got_ref)
    size = acc.shape[0] // PARTS
    copies = part_copies(acc, out_ref, sems)
    for i, copy in enumerate(copies):
        part = slice(i * size, (i + 1) * size)
        acc[part] = base_ref[part] + albedo_ref[part] * acc[part]
        copy.start()
    for copy in copies:
        copy.wait()


def last(asked_other, own_sum, got, base, albedo):
    return pl.pallas_call(
        last_kernel,
        in_specs=[SMEM_SPEC] + [VMEM_SPEC] * 4,
        out_specs=HBM_SPEC,
        out_shape=jax.ShapeDtypeStruct(base.shape, jnp.float32),
        scratch_shapes=[
            pltpu.VMEM(base.shape, jnp.float32),
            pltpu.SemaphoreType.DMA((PARTS,)),
        ],
        compiler_params=pltpu.CompilerParams(vmem_limit_bytes=VMEM // 4),
    )(asked_other, own_sum, got, base, albedo)


def ask_kernel(core_ref, fetch_ref, out_ref):
    core = core_ref[0]
    for owner in range(out_ref.shape[0]):
        out_ref[owner] = jnp.full((1, BLOCK), fetch_ref[2 * owner + core], jnp.int32)


def ask(core, fetch_block, owners):
    return pl.pallas_call(
        ask_kernel,
        in_specs=[SMEM_SPEC] * 2,
        out_specs=VMEM_SPEC,
        out_shape=jax.ShapeDtypeStruct((owners, 1, BLOCK), jnp.int32),
    )(core.reshape(1), fetch_block)


def part_copies(source, target, sems):
    size = source.shape[0] // PARTS
    return [
        pltpu.make_async_copy(
            source.at[pl.ds(i * size, size)], target.at[pl.ds(i * size, size)], sems.at[i]
        )
        for i in range(PARTS)
    ]


def put_asked(asked_ref, ex_ref, send, copies):
    size = send.shape[0] // PARTS

    def put(at, carry):
        send[at] = ex_ref[asked_ref[at]]
        return carry

    for i, copy in enumerate(copies):
        lax.fori_loop(i * size, (i + 1) * size, put, 0, unroll=8)
        copy.start()


def place_kernel(
    asked_ref, geometry_ref, place_ref, short_ref, placed, sems, short, short_sem, geometry, geometry_sem
):
    to_rows = pltpu.make_async_copy(geometry_ref, geometry, geometry_sem)
    to_rows.start()
    asked = asked_ref[...]
    row = lax.broadcasted_iota(jnp.int32, asked.shape, 0)
    column = lax.broadcasted_iota(jnp.int32, asked.shape, 1)
    short_ref[...] = jnp.sum(jnp.where(row == column, asked, 0), axis=0, keepdims=True)
    to_scalars = pltpu.make_async_copy(short_ref, short, short_sem)
    to_scalars.start()
    to_scalars.wait()
    to_rows.wait()

    def put(at, carry):
        placed[at] = geometry[pl.ds(short[0, at], 1), :]
        return carry

    copies = part_copies(placed, place_ref, sems)
    size = placed.shape[0] // PARTS
    for i, copy in enumerate(copies):
        lax.fori_loop(i * size, (i + 1) * size, put, 0, unroll=8)
        copy.start()
    for copy in copies:
        copy.wait()


def place(asked, geometry):
    owners = asked.shape[0]
    return pl.pallas_call(
        place_kernel,
        in_specs=[VMEM_SPEC, HBM_SPEC],
        out_specs=[HBM_SPEC, VMEM_SPEC],
        out_shape=[
            jax.ShapeDtypeStruct((owners, 1, geometry.shape[1]), jnp.float32),
            jax.ShapeDtypeStruct((1, owners), jnp.int32),
        ],
        scratch_shapes=[
            pltpu.VMEM((owners, 1, geometry.shape[1]), jnp.float32),
            pltpu.SemaphoreType.DMA((PARTS,)),
            pltpu.SMEM((1, owners), jnp.int32),
            pltpu.SemaphoreType.DMA,
            pltpu.VMEM(geometry.shape, jnp.float32),
            pltpu.SemaphoreType.DMA,
        ],
        compiler_params=pltpu.CompilerParams(vmem_limit_bytes=VMEM // 4),
    )(asked, geometry)


def first_kernel(asked_ref, area_ref, emission_ref, ex_out_ref, send_ref, ex, send, ex_sems, send_sems):
    ex[...] = (area_ref[...] * emission_ref[...]).astype(jnp.bfloat16)
    ex_copies = part_copies(ex, ex_out_ref, ex_sems)
    send_copies = part_copies(send, send_ref, send_sems)
    put_asked(asked_ref, ex, send, send_copies)
    for copy in ex_copies:
        copy.start()
    for copy in ex_copies + send_copies:
        copy.wait()


def first(asked, area, emission):
    blocks, hours, block = emission.shape
    owners = asked.shape[0]
    return pl.pallas_call(
        first_kernel,
        in_specs=[SMEM_SPEC] + [VMEM_SPEC] * 2,
        out_specs=[HBM_SPEC] * 2,
        out_shape=[
            pltpu.HBM((blocks, hours, block), jnp.bfloat16),
            pltpu.HBM((owners, hours, block), jnp.bfloat16),
        ],
        scratch_shapes=[
            pltpu.VMEM((blocks, hours, block), jnp.bfloat16),
            pltpu.VMEM((owners, hours, block), jnp.bfloat16),
            pltpu.SemaphoreType.DMA((PARTS,)),
            pltpu.SemaphoreType.DMA((PARTS,)),
        ],
        compiler_params=pltpu.CompilerParams(vmem_limit_bytes=VMEM // 4),
        cost_estimate=pl.CostEstimate(flops=10_000_000, bytes_accessed=8_000_000, transcendentals=0),
    )(asked, area, emission)


def factor_rows(x, y, z, area, facing, near):
    x, y, z = x - 3.0, y - 3.0, z - 3.0
    unit = (math.pi if near else 1.0) / facing
    norm = unit * (x * x + y * y + z * z + area)
    if near:
        terms = (norm, unit, -2.0 * unit * x, -2.0 * unit * y, -2.0 * unit * z)
        order = (0, 0, 1, 1, 0, 2)
    else:
        terms = (unit, norm, unit * x, unit * y, unit * z)
        order = (0, 1, 0, 1, 2, 0)
    found = []
    for term in terms:
        parts = []
        for _ in range(3):
            part = term.astype(jnp.bfloat16).astype(jnp.float32)
            parts.append(part)
            term = term - part
        found += [parts[i] for i in order]
    return found + [jnp.zeros_like(x)] * (FEATURES - len(found))


def factor_blocks(read, count, turned, near, put):
    def group(at, carry):
        for i, feature in enumerate(factor_rows(*read(pl.ds(pl.multiple_of(at * 8, 8), 8)), near)):
            turned[8 * i : 8 * i + 8, :] = feature
        for i in range(8):
            put(at * 8 + i, turned[pl.ds(i, FEATURES, stride=8), :])
        return carry

    lax.fori_loop(0, count // 8, group, 0)


def near_kernel(positions_ref, area_ref, facing_ref, out_ref, geometry_ref, turned):
    parts = [positions_ref[i] for i in range(3)] + [area_ref[...], facing_ref[...]]
    for i, part in enumerate(parts):
        geometry_ref[:, i * BLOCK : (i + 1) * BLOCK] = part

    def read(at):
        return [positions_ref[i, at, :] for i in range(3)] + [area_ref[at, :], facing_ref[at, :]]

    def put(at, block):
        out_ref[at] = block.T.astype(jnp.bfloat16)

    factor_blocks(read, out_ref.shape[0], turned, True, put)


def far_factors(geometry_ref, out, turned):
    def read(at):
        return [geometry_ref[at, 0, i * BLOCK : (i + 1) * BLOCK] for i in range(5)]

    def put(at, block):
        out[at] = block.astype(jnp.bfloat16)

    factor_blocks(read, out.shape[0], turned, False, put)


def near_factors(positions, patch_area, facing):
    blocks = patch_area.shape[0]
    return pl.pallas_call(
        near_kernel,
        in_specs=[VMEM_SPEC] * 3,
        out_specs=[VMEM_SPEC] * 2,
        out_shape=[
            jax.ShapeDtypeStruct((blocks, BLOCK, FEATURES), jnp.bfloat16),
            jax.ShapeDtypeStruct((blocks, 5 * BLOCK), jnp.float32),
        ],
        scratch_shapes=[pltpu.VMEM((8 * FEATURES, BLOCK), jnp.float32)],
        compiler_params=pltpu.CompilerParams(vmem_limit_bytes=VMEM),
        cost_estimate=pl.CostEstimate(flops=10_000_000, bytes_accessed=8_000_000, transcendentals=0),
    )(positions, patch_area, facing)


def local(
    emission, positions, patch_area, facing, albedo_class, albedo_table, fetch_block,
    pair_rows, pair_slots, pair_code,
):
    blocks, hours = emission.shape[:2]
    owners = lax.axis_size("blk")
    core = lax.axis_index("grp")

    def exchange(array):
        return lax.all_to_all(array, "blk", split_axis=0, concat_axis=0, tiled=True)

    def swap(array):
        return lax.ppermute(array, "grp", [(0, 1), (1, 0)])

    asked_rows = exchange(ask(core, fetch_block, owners)).reshape(owners, BLOCK)
    near, own_geometry = near_factors(positions, patch_area, facing)
    placed, asked = place(asked_rows, own_geometry)
    asked = asked.reshape(owners)
    geometry = exchange(placed)

    def words(pair_row, pair_slot, code):
        skip = (pair_slot & 1) ^ core
        return pair_row | (skip << 6) | ((pair_slot >> 1) << 7) | jnp.left_shift(code, 15)

    lists = (pair_rows, pair_slots, pair_code)
    pairs, steps = pair_list(words(*lists), words(*map(swap, lists)))
    area = patch_area[:, None, :]
    exitance, send = first(asked, area, emission)
    send, geometry, near, pairs, steps = lax.optimization_barrier((send, geometry, near, pairs, steps))

    class_ids = jnp.arange(NCLASS, dtype=jnp.int32)
    albedo = jnp.sum(
        jnp.where(albedo_class[..., None] == class_ids, albedo_table, jnp.float32(0.0)), axis=-1
    )[:, None, :]

    fetched = exchange(send)
    asked_other, geometry = lax.optimization_barrier((swap(asked), geometry))
    tiles, back = build(
        pairs, steps, jnp.asarray(hash_pattern()), near, geometry, exitance, 2 * pair_rows.shape[0]
    )

    def collect(back, fetched):
        got = exchange(back)
        to_rows = rows(pairs, steps, tiles, fetched, blocks)
        base = emission + albedo * (to_rows[:blocks] + swap(to_rows)[:blocks])
        got, base = lax.optimization_barrier((got, base))
        return own(asked, got, blocks), swap(got), base

    exitance, send = middle(asked, asked_other, *collect(back, fetched), albedo, area)
    fetched = exchange(send)
    back = columns(pairs, steps, tiles, exitance, owners)
    return last(asked_other, *collect(back, fetched), albedo)


def solution(mesh):
    in_specs = (
        P("blk", None, None),
        P(None, "blk", None),
        P("blk", None),
        P("blk", None),
        P("blk", None),
        P(),
        P("blk"),
        P(("blk", "grp")),
        P(("blk", "grp")),
        P(("blk", "grp")),
    )
    out_specs = P("blk", None, None)
    return jax.shard_map(local, mesh=mesh, in_specs=in_specs, out_specs=out_specs, check_vma=False)
```

```python
import math

import jax
import jax.numpy as jnp
import numpy as np
from jax import lax
from jax.experimental import pallas as pl
from jax.experimental.pallas import tpu as pltpu
from jax.sharding import PartitionSpec as P

BLOCK = 128
NCLASS = 8
HASH = 747796405
FEATURES = 32
UNROLL = 64
DEPTH = 4
VMEM = 60 * 1024 * 1024
SMEM_SPEC = pl.BlockSpec(memory_space=pltpu.SMEM)
VMEM_SPEC = pl.BlockSpec(memory_space=pltpu.VMEM)
ANY_SPEC = pl.BlockSpec(memory_space=pl.ANY)
HBM_SPEC = pl.BlockSpec(memory_space=pltpu.HBM)
PARTS = 4

SPARE = 64 | (128 << 7)


def hash_pattern():
    at = (np.arange(BLOCK * BLOCK, dtype=np.uint64) * HASH) & 0xFFFFFFFF
    odd = (at >> 2) ^ (at >> 6) ^ (at >> 7) ^ (at >> 11)
    word = (((at >> 14) << 21) + ((odd & 1) << 31)) & 0xFFFFFFFF
    return word.astype(np.uint32).astype(np.int32).reshape(BLOCK, BLOCK)


def row_of(word):
    return word & 127


def slot_of(word):
    return lax.shift_right_logical(word, jnp.int32(7)) & 255


def list_kernel(mine_ref, other_ref, list_ref, steps_ref):
    def take_from(words_ref):
        def take(turn, count):
            for j in range(8):
                word = words_ref[turn * 8 + j]
                list_ref[count] = word
                count = count + 1 - (lax.shift_right_logical(word, jnp.int32(6)) & 1)
            return count

        return take

    turns = mine_ref.shape[0] // 8
    count = lax.fori_loop(0, turns, take_from(mine_ref), jnp.int32(0))
    count = lax.fori_loop(0, turns, take_from(other_ref), count)
    for j in range(UNROLL):
        list_ref[count + j] = jnp.int32(SPARE)
    steps_ref[0] = jnp.maximum((count + UNROLL - 1) // UNROLL, 1)


def pair_list(mine, other):
    return pl.pallas_call(
        list_kernel,
        out_shape=(
            jax.ShapeDtypeStruct((2 * mine.shape[0] + UNROLL,), jnp.int32),
            jax.ShapeDtypeStruct((1,), jnp.int32),
        ),
        in_specs=[SMEM_SPEC] * 2,
        out_specs=(SMEM_SPEC,) * 2,
        cost_estimate=pl.CostEstimate(flops=10_000_000, bytes_accessed=10_000_000, transcendentals=0),
    )(mine, other)


def encode(acc, out_ref):
    def one(slot, carry):
        value = acc[slot]
        top = jnp.max(value, axis=0, keepdims=True)
        exponent = jnp.ceil(jnp.log2(jnp.maximum(top, 1e-30)))
        level = jnp.minimum(jnp.round(value * jnp.exp2(15.0 - exponent)), 32767.0).astype(jnp.int32)
        biased = exponent.astype(jnp.int32) + 128
        places = lax.broadcasted_iota(jnp.int32, value.shape, 0)
        mark = jnp.where(places < 8, lax.shift_right_logical(biased, jnp.minimum(places, 8)) & 1, 0)
        out_ref[slot] = (level ^ -mark).astype(jnp.int16)
        return carry

    lax.fori_loop(0, out_ref.shape[0], one, 0, unroll=4)


def decode(code):
    code = code.astype(jnp.int32)
    head = code[:8]
    places = lax.broadcasted_iota(jnp.int32, head.shape, 0)
    bits = jnp.where(head < 0, jnp.left_shift(jnp.ones_like(head), places), 0).astype(jnp.float32)
    biased = jnp.sum(bits, axis=0, keepdims=True)
    level = code ^ lax.shift_right_arithmetic(code, jnp.full_like(code, 31))
    return level.astype(jnp.float32) * jnp.exp2(biased - (128.0 + 15.0))


def tile_copy(tiles_ref, held, sems, step, out):
    buffer = lax.rem(step, DEPTH)
    away = tiles_ref.at[pl.ds(step * UNROLL, UNROLL)]
    here = held.at[buffer]
    source, target = (here, away) if out else (away, here)
    return pltpu.make_async_copy(source, target, sems.at[buffer])


def build_kernel(
    list_ref, steps_ref, pattern_ref, near_ref, geometry_ref, ex_ref, tiles_ref, out_ref,
    acc, held, sems, far, turned,
):
    steps = steps_ref[0]
    far_factors(geometry_ref, far, turned)
    acc[...] = jnp.zeros_like(acc)

    def turn(step, carry):
        buffer = lax.rem(step, DEPTH)

        @pl.when(step >= DEPTH)
        def _():
            tile_copy(tiles_ref, held, sems, step - DEPTH, True).wait()

        for j in range(UNROLL):
            word = list_ref[step * UNROLL + j]
            row, slot = row_of(word) & 63, slot_of(word)
            shift = jnp.left_shift(lax.shift_right_logical(word, jnp.int32(15)) * jnp.int32(HASH), 21)
            scaled = jnp.dot(near_ref[row], far[slot & 127], preferred_element_type=jnp.float32)
            mixed = pattern_ref[...] + shift
            mixed = mixed ^ jnp.left_shift(mixed, 5)
            tile = jnp.where(mixed < 0, pl.reciprocal(scaled, approx=True), 0.0).astype(jnp.bfloat16)
            held[buffer, j] = tile
            acc[slot] += jnp.dot(ex_ref[row], tile, preferred_element_type=jnp.float32)
        tile_copy(tiles_ref, held, sems, step, True).start()
        return carry

    lax.fori_loop(0, steps, turn, 0)
    encode(acc, out_ref)

    def drain(step, carry):
        tile_copy(tiles_ref, held, sems, step, True).wait()
        return carry

    lax.fori_loop(jnp.maximum(steps - DEPTH, 0), steps, drain, 0)


def stream(steps, tiles_ref, held, sems, use):
    def fetch(step, carry):
        tile_copy(tiles_ref, held, sems, step, False).start()
        return carry

    lax.fori_loop(0, jnp.minimum(steps, DEPTH - 1), fetch, 0)

    def turn(step, carry):
        @pl.when(step + DEPTH - 1 < steps)
        def _():
            fetch(step + DEPTH - 1, 0)

        tile_copy(tiles_ref, held, sems, step, False).wait()
        use(step, lax.rem(step, DEPTH))
        return carry

    lax.fori_loop(0, steps, turn, 0)


def columns_kernel(list_ref, steps_ref, tiles_ref, ex_ref, out_ref, acc, held, sems):
    acc[...] = jnp.zeros_like(acc)

    def use(step, buffer):
        for j in range(UNROLL):
            word = list_ref[step * UNROLL + j]
            row, slot = row_of(word) & 63, slot_of(word)
            acc[slot] += jnp.dot(ex_ref[row], held[buffer, j], preferred_element_type=jnp.float32)

    stream(steps_ref[0], tiles_ref, held, sems, use)
    encode(acc, out_ref)


def rows_kernel(list_ref, steps_ref, tiles_ref, ex_ref, out_ref, held, sems):
    out_ref[...] = jnp.zeros_like(out_ref)

    def use(step, buffer):
        for j in range(UNROLL):
            word = list_ref[step * UNROLL + j]
            row, slot = row_of(word), slot_of(word) & 127
            out_ref[row] += lax.dot_general(
                ex_ref[slot], held[buffer, j], (((1,), (1,)), ((), ())),
                preferred_element_type=jnp.float32,
            )

    stream(steps_ref[0], tiles_ref, held, sems, use)


HELD = pltpu.VMEM((DEPTH, UNROLL, BLOCK, BLOCK), jnp.bfloat16)
SEMS = pltpu.SemaphoreType.DMA((DEPTH,))


def build(pairs, steps, pattern, near, geometry, exitance, pair_max):
    slots, hours = geometry.shape[0], exitance.shape[1]
    return pl.pallas_call(
        build_kernel,
        in_specs=[SMEM_SPEC] * 2 + [VMEM_SPEC] * 4,
        out_specs=[ANY_SPEC, VMEM_SPEC],
        out_shape=[
            jax.ShapeDtypeStruct((pair_max, BLOCK, BLOCK), jnp.bfloat16),
            jax.ShapeDtypeStruct((slots, hours, BLOCK), jnp.int16),
        ],
        scratch_shapes=[
            pltpu.VMEM((slots + 1, hours, BLOCK), jnp.float32),
            HELD,
            SEMS,
            pltpu.VMEM((slots, FEATURES, BLOCK), jnp.bfloat16),
            pltpu.VMEM((8 * FEATURES, BLOCK), jnp.float32),
        ],
        compiler_params=pltpu.CompilerParams(vmem_limit_bytes=VMEM),
        cost_estimate=pl.CostEstimate(
            flops=20_000_000_000, bytes_accessed=60_000_000, transcendentals=10_000_000
        ),
    )(pairs, steps, pattern, near, geometry, exitance)


def columns(pairs, steps, tiles, exitance, slots):
    hours = exitance.shape[1]
    return pl.pallas_call(
        columns_kernel,
        in_specs=[SMEM_SPEC] * 2 + [ANY_SPEC, VMEM_SPEC],
        out_specs=VMEM_SPEC,
        out_shape=jax.ShapeDtypeStruct((slots, hours, BLOCK), jnp.int16),
        scratch_shapes=[pltpu.VMEM((slots + 1, hours, BLOCK), jnp.float32), HELD, SEMS],
        compiler_params=pltpu.CompilerParams(vmem_limit_bytes=VMEM),
        cost_estimate=pl.CostEstimate(flops=10_000_000_000, bytes_accessed=40_000_000, transcendentals=0),
    )(pairs, steps, tiles, exitance)


def rows(pairs, steps, tiles, fetched, row_blocks):
    hours = fetched.shape[1]
    return pl.pallas_call(
        rows_kernel,
        in_specs=[SMEM_SPEC] * 2 + [ANY_SPEC, VMEM_SPEC],
        out_specs=VMEM_SPEC,
        out_shape=jax.ShapeDtypeStruct((row_blocks + 1, hours, BLOCK), jnp.float32),
        scratch_shapes=[HELD, SEMS],
        compiler_params=pltpu.CompilerParams(vmem_limit_bytes=VMEM),
        cost_estimate=pl.CostEstimate(flops=10_000_000_000, bytes_accessed=40_000_000, transcendentals=0),
    )(pairs, steps, tiles, fetched)


def add_asked(acc, asked_ref, got_ref):
    def add(at, carry):
        acc[asked_ref[at]] += decode(got_ref[at])
        return carry

    lax.fori_loop(0, got_ref.shape[0], add, 0, unroll=8)


def own_kernel(asked_ref, got_ref, out_ref):
    out_ref[...] = jnp.zeros_like(out_ref)
    add_asked(out_ref, asked_ref, got_ref)


def own(asked, got, blocks):
    return pl.pallas_call(
        own_kernel,
        in_specs=[SMEM_SPEC, VMEM_SPEC],
        out_specs=VMEM_SPEC,
        out_shape=jax.ShapeDtypeStruct((blocks,) + got.shape[1:], jnp.float32),
        compiler_params=pltpu.CompilerParams(vmem_limit_bytes=VMEM // 4),
        cost_estimate=pl.CostEstimate(flops=10_000_000, bytes_accessed=4_000_000, transcendentals=0),
    )(asked, got)


def middle_kernel(
    asked_ref, asked_other_ref, own_ref, got_ref, base_ref, albedo_ref, area_ref, ex_out_ref, send_ref,
    acc, ex, send, ex_sems, send_sems,
):
    acc[...] = own_ref[...]
    add_asked(acc, asked_other_ref, got_ref)
    ex[...] = (area_ref[...] * (base_ref[...] + albedo_ref[...] * acc[...])).astype(jnp.bfloat16)
    send_copies = part_copies(send, send_ref, send_sems)
    ex_copies = part_copies(ex, ex_out_ref, ex_sems)
    put_asked(asked_ref, ex, send, send_copies)
    for copy in ex_copies:
        copy.start()
    for copy in ex_copies + send_copies:
        copy.wait()


def middle(asked, asked_other, own_sum, got, base, albedo, area):
    blocks, hours, block = base.shape
    owners = asked.shape[0]
    return pl.pallas_call(
        middle_kernel,
        in_specs=[SMEM_SPEC] * 2 + [VMEM_SPEC] * 5,
        out_specs=[HBM_SPEC] * 2,
        out_shape=[
            pltpu.HBM((blocks, hours, block), jnp.bfloat16),
            pltpu.HBM((owners, hours, block), jnp.bfloat16),
        ],
        scratch_shapes=[
            pltpu.VMEM((blocks, hours, block), jnp.float32),
            pltpu.VMEM((blocks, hours, block), jnp.bfloat16),
            pltpu.VMEM((owners, hours, block), jnp.bfloat16),
            pltpu.SemaphoreType.DMA((PARTS,)),
            pltpu.SemaphoreType.DMA((PARTS,)),
        ],
        compiler_params=pltpu.CompilerParams(vmem_limit_bytes=VMEM // 4),
    )(asked, asked_other, own_sum, got, base, albedo, area)


def last_kernel(asked_other_ref, own_ref, got_ref, base_ref, albedo_ref, out_ref, acc, sems):
    acc[...] = own_ref[...]
    add_asked(acc, asked_other_ref, got_ref)
    size = acc.shape[0] // PARTS
    copies = part_copies(acc, out_ref, sems)
    for i, copy in enumerate(copies):
        part = slice(i * size, (i + 1) * size)
        acc[part] = base_ref[part] + albedo_ref[part] * acc[part]
        copy.start()
    for copy in copies:
        copy.wait()


def last(asked_other, own_sum, got, base, albedo):
    return pl.pallas_call(
        last_kernel,
        in_specs=[SMEM_SPEC] + [VMEM_SPEC] * 4,
        out_specs=HBM_SPEC,
        out_shape=jax.ShapeDtypeStruct(base.shape, jnp.float32),
        scratch_shapes=[
            pltpu.VMEM(base.shape, jnp.float32),
            pltpu.SemaphoreType.DMA((PARTS,)),
        ],
        compiler_params=pltpu.CompilerParams(vmem_limit_bytes=VMEM // 4),
    )(asked_other, own_sum, got, base, albedo)


def ask_kernel(core_ref, fetch_ref, out_ref):
    core = core_ref[0]
    for owner in range(out_ref.shape[0]):
        out_ref[owner] = jnp.full((1, BLOCK), fetch_ref[2 * owner + core], jnp.int32)


def ask(core, fetch_block, owners):
    return pl.pallas_call(
        ask_kernel,
        in_specs=[SMEM_SPEC] * 2,
        out_specs=VMEM_SPEC,
        out_shape=jax.ShapeDtypeStruct((owners, 1, BLOCK), jnp.int32),
    )(core.reshape(1), fetch_block)


def part_copies(source, target, sems):
    size = source.shape[0] // PARTS
    return [
        pltpu.make_async_copy(
            source.at[pl.ds(i * size, size)], target.at[pl.ds(i * size, size)], sems.at[i]
        )
        for i in range(PARTS)
    ]


def put_asked(asked_ref, ex_ref, send, copies):
    size = send.shape[0] // PARTS

    def put(at, carry):
        send[at] = ex_ref[asked_ref[at]]
        return carry

    for i, copy in enumerate(copies):
        lax.fori_loop(i * size, (i + 1) * size, put, 0, unroll=8)
        copy.start()


def place_kernel(asked_ref, geometry_ref, place_ref, short_ref, placed, sems, short, short_sem):
    asked = asked_ref[...]
    row = lax.broadcasted_iota(jnp.int32, asked.shape, 0)
    column = lax.broadcasted_iota(jnp.int32, asked.shape, 1)
    short_ref[...] = jnp.sum(jnp.where(row == column, asked, 0), axis=0, keepdims=True)
    to_scalars = pltpu.make_async_copy(short_ref, short, short_sem)
    to_scalars.start()
    to_scalars.wait()

    def put(at, carry):
        placed[at] = geometry_ref[pl.ds(short[0, at], 1), :]
        return carry

    copies = part_copies(placed, place_ref, sems)
    size = placed.shape[0] // PARTS
    for i, copy in enumerate(copies):
        lax.fori_loop(i * size, (i + 1) * size, put, 0, unroll=8)
        copy.start()
    for copy in copies:
        copy.wait()


def place(asked, geometry):
    owners = asked.shape[0]
    return pl.pallas_call(
        place_kernel,
        in_specs=[VMEM_SPEC] * 2,
        out_specs=[HBM_SPEC, VMEM_SPEC],
        out_shape=[
            jax.ShapeDtypeStruct((owners, 1, geometry.shape[1]), jnp.float32),
            jax.ShapeDtypeStruct((1, owners), jnp.int32),
        ],
        scratch_shapes=[
            pltpu.VMEM((owners, 1, geometry.shape[1]), jnp.float32),
            pltpu.SemaphoreType.DMA((PARTS,)),
            pltpu.SMEM((1, owners), jnp.int32),
            pltpu.SemaphoreType.DMA,
        ],
        compiler_params=pltpu.CompilerParams(vmem_limit_bytes=VMEM // 4),
    )(asked, geometry)


def first_kernel(asked_ref, area_ref, emission_ref, ex_out_ref, send_ref, ex, send, ex_sems, send_sems):
    ex[...] = (area_ref[...] * emission_ref[...]).astype(jnp.bfloat16)
    ex_copies = part_copies(ex, ex_out_ref, ex_sems)
    send_copies = part_copies(send, send_ref, send_sems)
    put_asked(asked_ref, ex, send, send_copies)
    for copy in ex_copies:
        copy.start()
    for copy in ex_copies + send_copies:
        copy.wait()


def first(asked, area, emission):
    blocks, hours, block = emission.shape
    owners = asked.shape[0]
    return pl.pallas_call(
        first_kernel,
        in_specs=[SMEM_SPEC] + [VMEM_SPEC] * 2,
        out_specs=[HBM_SPEC] * 2,
        out_shape=[
            pltpu.HBM((blocks, hours, block), jnp.bfloat16),
            pltpu.HBM((owners, hours, block), jnp.bfloat16),
        ],
        scratch_shapes=[
            pltpu.VMEM((blocks, hours, block), jnp.bfloat16),
            pltpu.VMEM((owners, hours, block), jnp.bfloat16),
            pltpu.SemaphoreType.DMA((PARTS,)),
            pltpu.SemaphoreType.DMA((PARTS,)),
        ],
        compiler_params=pltpu.CompilerParams(vmem_limit_bytes=VMEM // 4),
        cost_estimate=pl.CostEstimate(flops=10_000_000, bytes_accessed=8_000_000, transcendentals=0),
    )(asked, area, emission)


def factor_rows(x, y, z, area, facing, near):
    x, y, z = x - 3.0, y - 3.0, z - 3.0
    unit = (math.pi if near else 1.0) / facing
    norm = unit * (x * x + y * y + z * z + area)
    if near:
        terms = (norm, unit, -2.0 * unit * x, -2.0 * unit * y, -2.0 * unit * z)
        order = (0, 0, 1, 1, 0, 2)
    else:
        terms = (unit, norm, unit * x, unit * y, unit * z)
        order = (0, 1, 0, 1, 2, 0)
    found = []
    for term in terms:
        parts = []
        for _ in range(3):
            part = term.astype(jnp.bfloat16).astype(jnp.float32)
            parts.append(part)
            term = term - part
        found += [parts[i] for i in order]
    return found + [jnp.zeros_like(x)] * (FEATURES - len(found))


def factor_blocks(read, count, turned, near, put):
    def group(at, carry):
        for i, feature in enumerate(factor_rows(*read(pl.ds(pl.multiple_of(at * 8, 8), 8)), near)):
            turned[8 * i : 8 * i + 8, :] = feature
        for i in range(8):
            put(at * 8 + i, turned[pl.ds(i, FEATURES, stride=8), :])
        return carry

    lax.fori_loop(0, count // 8, group, 0)


def near_kernel(positions_ref, area_ref, facing_ref, out_ref, geometry_ref, turned, made, sems):
    parts = [positions_ref[i] for i in range(3)] + [area_ref[...], facing_ref[...]]
    for i, part in enumerate(parts):
        geometry_ref[:, i * BLOCK : (i + 1) * BLOCK] = part

    def read(at):
        return [positions_ref[i, at, :] for i in range(3)] + [area_ref[at, :], facing_ref[at, :]]

    def put(at, block):
        made[at] = block.T.astype(jnp.bfloat16)

    factor_blocks(read, made.shape[0], turned, True, put)
    copies = part_copies(made, out_ref, sems)
    for copy in copies:
        copy.start()
    for copy in copies:
        copy.wait()


def far_factors(geometry_ref, out, turned):
    def read(at):
        return [geometry_ref[at, 0, i * BLOCK : (i + 1) * BLOCK] for i in range(5)]

    def put(at, block):
        out[at] = block.astype(jnp.bfloat16)

    factor_blocks(read, out.shape[0], turned, False, put)


def near_factors(positions, patch_area, facing):
    blocks = patch_area.shape[0]
    return pl.pallas_call(
        near_kernel,
        in_specs=[VMEM_SPEC] * 3,
        out_specs=[HBM_SPEC, VMEM_SPEC],
        out_shape=[
            pltpu.HBM((blocks, BLOCK, FEATURES), jnp.bfloat16),
            jax.ShapeDtypeStruct((blocks, 5 * BLOCK), jnp.float32),
        ],
        scratch_shapes=[
            pltpu.VMEM((8 * FEATURES, BLOCK), jnp.float32),
            pltpu.VMEM((blocks, BLOCK, FEATURES), jnp.bfloat16),
            pltpu.SemaphoreType.DMA((PARTS,)),
        ],
        compiler_params=pltpu.CompilerParams(vmem_limit_bytes=VMEM // 4),
        cost_estimate=pl.CostEstimate(flops=10_000_000, bytes_accessed=8_000_000, transcendentals=0),
    )(positions, patch_area, facing)


def local(
    emission, positions, patch_area, facing, albedo_class, albedo_table, fetch_block,
    pair_rows, pair_slots, pair_code,
):
    blocks, hours = emission.shape[:2]
    owners = lax.axis_size("blk")
    core = lax.axis_index("grp")

    def exchange(array):
        return lax.all_to_all(array, "blk", split_axis=0, concat_axis=0, tiled=True)

    def swap(array):
        return lax.ppermute(array, "grp", [(0, 1), (1, 0)])

    asked_rows = exchange(ask(core, fetch_block, owners)).reshape(owners, BLOCK)
    near, own_geometry = near_factors(positions, patch_area, facing)
    placed, asked = place(asked_rows, own_geometry)
    asked = asked.reshape(owners)
    geometry = exchange(placed)

    def words(pair_row, pair_slot, code):
        skip = (pair_slot & 1) ^ core
        return pair_row | (skip << 6) | ((pair_slot >> 1) << 7) | jnp.left_shift(code, 15)

    lists = (pair_rows, pair_slots, pair_code)
    pairs, steps = pair_list(words(*lists), words(*map(swap, lists)))
    area = patch_area[:, None, :]
    exitance, send = first(asked, area, emission)
    send, geometry, near, pairs, steps = lax.optimization_barrier((send, geometry, near, pairs, steps))

    class_ids = jnp.arange(NCLASS, dtype=jnp.int32)
    albedo = jnp.sum(
        jnp.where(albedo_class[..., None] == class_ids, albedo_table, jnp.float32(0.0)), axis=-1
    )[:, None, :]

    fetched = exchange(send)
    tiles, back = build(
        pairs, steps, jnp.asarray(hash_pattern()), near, geometry, exitance, 2 * pair_rows.shape[0]
    )

    asked_other, back = lax.optimization_barrier((swap(asked), back))

    def collect(back, fetched):
        got = exchange(back)
        to_rows = rows(pairs, steps, tiles, fetched, blocks)
        base = emission + albedo * (to_rows[:blocks] + swap(to_rows)[:blocks])
        got, base = lax.optimization_barrier((got, base))
        return own(asked, got, blocks), swap(got), base

    exitance, send = middle(asked, asked_other, *collect(back, fetched), albedo, area)
    fetched = exchange(send)
    back = columns(pairs, steps, tiles, exitance, owners)
    return last(asked_other, *collect(back, fetched), albedo)


def solution(mesh):
    in_specs = (
        P("blk", None, None),
        P(None, "blk", None),
        P("blk", None),
        P("blk", None),
        P("blk", None),
        P(),
        P("blk"),
        P(("blk", "grp")),
        P(("blk", "grp")),
        P(("blk", "grp")),
    )
    out_specs = P("blk", None, None)
    return jax.shard_map(local, mesh=mesh, in_specs=in_specs, out_specs=out_specs, check_vma=False)
```

```python
import math

import jax
import jax.numpy as jnp
import numpy as np
from jax import lax
from jax.experimental import pallas as pl
from jax.experimental.pallas import tpu as pltpu
from jax.sharding import PartitionSpec as P

BLOCK = 128
NCLASS = 8
HASH = 747796405
FEATURES = 32
UNROLL = 64
DEPTH = 4
VMEM = 60 * 1024 * 1024
SMEM_SPEC = pl.BlockSpec(memory_space=pltpu.SMEM)
VMEM_SPEC = pl.BlockSpec(memory_space=pltpu.VMEM)
ANY_SPEC = pl.BlockSpec(memory_space=pl.ANY)
HBM_SPEC = pl.BlockSpec(memory_space=pltpu.HBM)
PARTS = 4

SPARE = 64 | (128 << 7)


def hash_pattern():
    at = (np.arange(BLOCK * BLOCK, dtype=np.uint64) * HASH) & 0xFFFFFFFF
    odd = (at >> 2) ^ (at >> 6) ^ (at >> 7) ^ (at >> 11)
    word = (((at >> 14) << 21) + ((odd & 1) << 31)) & 0xFFFFFFFF
    return word.astype(np.uint32).astype(np.int32).reshape(BLOCK, BLOCK)


def row_of(word):
    return word & 127


def slot_of(word):
    return lax.shift_right_logical(word, jnp.int32(7)) & 255


def list_kernel(mine_ref, other_ref, list_ref, steps_ref):
    def take_from(words_ref):
        def take(turn, count):
            for j in range(8):
                word = words_ref[turn * 8 + j]
                list_ref[count] = word
                count = count + 1 - (lax.shift_right_logical(word, jnp.int32(6)) & 1)
            return count

        return take

    turns = mine_ref.shape[0] // 8
    count = lax.fori_loop(0, turns, take_from(mine_ref), jnp.int32(0))
    count = lax.fori_loop(0, turns, take_from(other_ref), count)
    for j in range(UNROLL):
        list_ref[count + j] = jnp.int32(SPARE)
    steps_ref[0] = jnp.maximum((count + UNROLL - 1) // UNROLL, 1)


def pair_list(mine, other):
    return pl.pallas_call(
        list_kernel,
        out_shape=(
            jax.ShapeDtypeStruct((2 * mine.shape[0] + UNROLL,), jnp.int32),
            jax.ShapeDtypeStruct((1,), jnp.int32),
        ),
        in_specs=[SMEM_SPEC] * 2,
        out_specs=(SMEM_SPEC,) * 2,
        cost_estimate=pl.CostEstimate(flops=10_000_000, bytes_accessed=10_000_000, transcendentals=0),
    )(mine, other)


def encode(acc, out_ref):
    def one(slot, carry):
        value = acc[slot]
        top = jnp.max(value, axis=0, keepdims=True)
        exponent = jnp.ceil(jnp.log2(jnp.maximum(top, 1e-30)))
        level = jnp.minimum(jnp.round(value * jnp.exp2(15.0 - exponent)), 32767.0).astype(jnp.int32)
        biased = exponent.astype(jnp.int32) + 128
        places = lax.broadcasted_iota(jnp.int32, value.shape, 0)
        mark = jnp.where(places < 8, lax.shift_right_logical(biased, jnp.minimum(places, 8)) & 1, 0)
        out_ref[slot] = (level ^ -mark).astype(jnp.int16)
        return carry

    lax.fori_loop(0, out_ref.shape[0], one, 0, unroll=4)


def decode(code):
    code = code.astype(jnp.int32)
    head = code[:8]
    places = lax.broadcasted_iota(jnp.int32, head.shape, 0)
    bits = jnp.where(head < 0, jnp.left_shift(jnp.ones_like(head), places), 0).astype(jnp.float32)
    biased = jnp.sum(bits, axis=0, keepdims=True)
    level = code ^ lax.shift_right_arithmetic(code, jnp.full_like(code, 31))
    return level.astype(jnp.float32) * jnp.exp2(biased - (128.0 + 15.0))


def tile_copy(tiles_ref, held, sems, step, out):
    buffer = lax.rem(step, DEPTH)
    away = tiles_ref.at[pl.ds(step * UNROLL, UNROLL)]
    here = held.at[buffer]
    source, target = (here, away) if out else (away, here)
    return pltpu.make_async_copy(source, target, sems.at[buffer])


def build_kernel(
    list_ref, steps_ref, pattern_ref, near_ref, geometry_ref, ex_ref, tiles_ref, out_ref,
    acc, held, sems, far, turned,
):
    steps = steps_ref[0]
    far_factors(geometry_ref, far, turned)
    acc[...] = jnp.zeros_like(acc)

    def turn(step, carry):
        buffer = lax.rem(step, DEPTH)

        @pl.when(step >= DEPTH)
        def _():
            tile_copy(tiles_ref, held, sems, step - DEPTH, True).wait()

        for j in range(UNROLL):
            word = list_ref[step * UNROLL + j]
            row, slot = row_of(word) & 63, slot_of(word)
            shift = jnp.left_shift(lax.shift_right_logical(word, jnp.int32(15)) * jnp.int32(HASH), 21)
            scaled = jnp.dot(near_ref[row], far[slot & 127], preferred_element_type=jnp.float32)
            mixed = pattern_ref[...] + shift
            mixed = mixed ^ jnp.left_shift(mixed, 5)
            tile = jnp.where(mixed < 0, pl.reciprocal(scaled, approx=True), 0.0).astype(jnp.bfloat16)
            held[buffer, j] = tile
            acc[slot] += jnp.dot(ex_ref[row], tile, preferred_element_type=jnp.float32)
        tile_copy(tiles_ref, held, sems, step, True).start()
        return carry

    lax.fori_loop(0, steps, turn, 0)
    encode(acc, out_ref)

    def drain(step, carry):
        tile_copy(tiles_ref, held, sems, step, True).wait()
        return carry

    lax.fori_loop(jnp.maximum(steps - DEPTH, 0), steps, drain, 0)


def stream(steps, tiles_ref, held, sems, prepare, use):
    def fetch(step, carry):
        tile_copy(tiles_ref, held, sems, step, False).start()
        return carry

    fetch(0, 0)
    prepare()
    lax.fori_loop(1, jnp.minimum(steps, DEPTH - 1), fetch, 0)

    def turn(step, carry):
        @pl.when(step + DEPTH - 1 < steps)
        def _():
            fetch(step + DEPTH - 1, 0)

        tile_copy(tiles_ref, held, sems, step, False).wait()
        use(step, lax.rem(step, DEPTH))
        return carry

    lax.fori_loop(0, steps, turn, 0)


def columns_kernel(list_ref, steps_ref, tiles_ref, ex_ref, out_ref, acc, held, sems):
    def prepare():
        acc[...] = jnp.zeros_like(acc)

    def use(step, buffer):
        for j in range(UNROLL):
            word = list_ref[step * UNROLL + j]
            row, slot = row_of(word) & 63, slot_of(word)
            acc[slot] += jnp.dot(ex_ref[row], held[buffer, j], preferred_element_type=jnp.float32)

    stream(steps_ref[0], tiles_ref, held, sems, prepare, use)
    encode(acc, out_ref)


def rows_kernel(list_ref, steps_ref, tiles_ref, fetched_ref, out_ref, held, sems, ex, ex_sem):
    def prepare():
        copy = pltpu.make_async_copy(fetched_ref, ex, ex_sem)
        copy.start()
        out_ref[...] = jnp.zeros_like(out_ref)
        copy.wait()

    def use(step, buffer):
        for j in range(UNROLL):
            word = list_ref[step * UNROLL + j]
            row, slot = row_of(word), slot_of(word) & 127
            out_ref[row] += lax.dot_general(
                ex[slot], held[buffer, j], (((1,), (1,)), ((), ())), preferred_element_type=jnp.float32
            )

    stream(steps_ref[0], tiles_ref, held, sems, prepare, use)


HELD = pltpu.VMEM((DEPTH, UNROLL, BLOCK, BLOCK), jnp.bfloat16)
SEMS = pltpu.SemaphoreType.DMA((DEPTH,))


def build(pairs, steps, pattern, near, geometry, exitance, pair_max):
    slots, hours = geometry.shape[0], exitance.shape[1]
    return pl.pallas_call(
        build_kernel,
        in_specs=[SMEM_SPEC] * 2 + [VMEM_SPEC] * 4,
        out_specs=[ANY_SPEC, VMEM_SPEC],
        out_shape=[
            jax.ShapeDtypeStruct((pair_max, BLOCK, BLOCK), jnp.bfloat16),
            jax.ShapeDtypeStruct((slots, hours, BLOCK), jnp.int16),
        ],
        scratch_shapes=[
            pltpu.VMEM((slots + 1, hours, BLOCK), jnp.float32),
            HELD,
            SEMS,
            pltpu.VMEM((slots, FEATURES, BLOCK), jnp.bfloat16),
            pltpu.VMEM((8 * FEATURES, BLOCK), jnp.float32),
        ],
        compiler_params=pltpu.CompilerParams(vmem_limit_bytes=VMEM),
        cost_estimate=pl.CostEstimate(
            flops=20_000_000_000, bytes_accessed=60_000_000, transcendentals=10_000_000
        ),
    )(pairs, steps, pattern, near, geometry, exitance)


def columns(pairs, steps, tiles, exitance, slots):
    hours = exitance.shape[1]
    return pl.pallas_call(
        columns_kernel,
        in_specs=[SMEM_SPEC] * 2 + [ANY_SPEC, VMEM_SPEC],
        out_specs=VMEM_SPEC,
        out_shape=jax.ShapeDtypeStruct((slots, hours, BLOCK), jnp.int16),
        scratch_shapes=[pltpu.VMEM((slots + 1, hours, BLOCK), jnp.float32), HELD, SEMS],
        compiler_params=pltpu.CompilerParams(vmem_limit_bytes=VMEM),
        cost_estimate=pl.CostEstimate(flops=10_000_000_000, bytes_accessed=40_000_000, transcendentals=0),
    )(pairs, steps, tiles, exitance)


def rows(pairs, steps, tiles, fetched, row_blocks):
    hours = fetched.shape[1]
    return pl.pallas_call(
        rows_kernel,
        in_specs=[SMEM_SPEC] * 2 + [ANY_SPEC, ANY_SPEC],
        out_specs=VMEM_SPEC,
        out_shape=jax.ShapeDtypeStruct((row_blocks + 1, hours, BLOCK), jnp.float32),
        scratch_shapes=[HELD, SEMS, pltpu.VMEM(fetched.shape, jnp.bfloat16), pltpu.SemaphoreType.DMA],
        compiler_params=pltpu.CompilerParams(vmem_limit_bytes=VMEM),
        cost_estimate=pl.CostEstimate(flops=10_000_000_000, bytes_accessed=40_000_000, transcendentals=0),
    )(pairs, steps, tiles, fetched)


def add_asked(acc, asked_ref, got_ref):
    def add(at, carry):
        acc[asked_ref[at]] += decode(got_ref[at])
        return carry

    lax.fori_loop(0, got_ref.shape[0], add, 0, unroll=8)


def own_kernel(asked_ref, got_ref, out_ref):
    out_ref[...] = jnp.zeros_like(out_ref)
    add_asked(out_ref, asked_ref, got_ref)


def own(asked, got, blocks):
    return pl.pallas_call(
        own_kernel,
        in_specs=[SMEM_SPEC, VMEM_SPEC],
        out_specs=VMEM_SPEC,
        out_shape=jax.ShapeDtypeStruct((blocks,) + got.shape[1:], jnp.float32),
        compiler_params=pltpu.CompilerParams(vmem_limit_bytes=VMEM // 4),
        cost_estimate=pl.CostEstimate(flops=10_000_000, bytes_accessed=4_000_000, transcendentals=0),
    )(asked, got)


def middle_kernel(
    asked_ref, asked_other_ref, own_ref, got_ref, base_ref, albedo_ref, area_ref, ex_out_ref, send_ref,
    acc, ex, send, ex_sems, send_sems,
):
    acc[...] = own_ref[...]
    add_asked(acc, asked_other_ref, got_ref)
    ex[...] = (area_ref[...] * (base_ref[...] + albedo_ref[...] * acc[...])).astype(jnp.bfloat16)
    send_copies = part_copies(send, send_ref, send_sems)
    ex_copies = part_copies(ex, ex_out_ref, ex_sems)
    put_asked(asked_ref, ex, send, send_copies)
    for copy in ex_copies:
        copy.start()
    for copy in ex_copies + send_copies:
        copy.wait()


def middle(asked, asked_other, own_sum, got, base, albedo, area):
    blocks, hours, block = base.shape
    owners = asked.shape[0]
    return pl.pallas_call(
        middle_kernel,
        in_specs=[SMEM_SPEC] * 2 + [VMEM_SPEC] * 5,
        out_specs=[HBM_SPEC] * 2,
        out_shape=[
            pltpu.HBM((blocks, hours, block), jnp.bfloat16),
            pltpu.HBM((owners, hours, block), jnp.bfloat16),
        ],
        scratch_shapes=[
            pltpu.VMEM((blocks, hours, block), jnp.float32),
            pltpu.VMEM((blocks, hours, block), jnp.bfloat16),
            pltpu.VMEM((owners, hours, block), jnp.bfloat16),
            pltpu.SemaphoreType.DMA((PARTS,)),
            pltpu.SemaphoreType.DMA((PARTS,)),
        ],
        compiler_params=pltpu.CompilerParams(vmem_limit_bytes=VMEM // 4),
    )(asked, asked_other, own_sum, got, base, albedo, area)


def last_kernel(asked_other_ref, own_ref, got_ref, base_ref, albedo_ref, out_ref, acc, sems):
    acc[...] = own_ref[...]
    add_asked(acc, asked_other_ref, got_ref)
    size = acc.shape[0] // PARTS
    copies = part_copies(acc, out_ref, sems)
    for i, copy in enumerate(copies):
        part = slice(i * size, (i + 1) * size)
        acc[part] = base_ref[part] + albedo_ref[part] * acc[part]
        copy.start()
    for copy in copies:
        copy.wait()


def last(asked_other, own_sum, got, base, albedo):
    return pl.pallas_call(
        last_kernel,
        in_specs=[SMEM_SPEC] + [VMEM_SPEC] * 4,
        out_specs=HBM_SPEC,
        out_shape=jax.ShapeDtypeStruct(base.shape, jnp.float32),
        scratch_shapes=[
            pltpu.VMEM(base.shape, jnp.float32),
            pltpu.SemaphoreType.DMA((PARTS,)),
        ],
        compiler_params=pltpu.CompilerParams(vmem_limit_bytes=VMEM // 4),
    )(asked_other, own_sum, got, base, albedo)


def ask_kernel(core_ref, fetch_ref, out_ref):
    core = core_ref[0]
    for owner in range(out_ref.shape[0]):
        out_ref[owner] = jnp.full((1, BLOCK), fetch_ref[2 * owner + core], jnp.int32)


def ask(core, fetch_block, owners):
    return pl.pallas_call(
        ask_kernel,
        in_specs=[SMEM_SPEC] * 2,
        out_specs=VMEM_SPEC,
        out_shape=jax.ShapeDtypeStruct((owners, 1, BLOCK), jnp.int32),
    )(core.reshape(1), fetch_block)


def part_copies(source, target, sems):
    size = source.shape[0] // PARTS
    return [
        pltpu.make_async_copy(
            source.at[pl.ds(i * size, size)], target.at[pl.ds(i * size, size)], sems.at[i]
        )
        for i in range(PARTS)
    ]


def put_asked(asked_ref, ex_ref, send, copies):
    size = send.shape[0] // PARTS

    def put(at, carry):
        send[at] = ex_ref[asked_ref[at]]
        return carry

    for i, copy in enumerate(copies):
        lax.fori_loop(i * size, (i + 1) * size, put, 0, unroll=8)
        copy.start()


def place_kernel(asked_ref, geometry_ref, place_ref, short_ref, placed, sems, short, short_sem):
    asked = asked_ref[...]
    row = lax.broadcasted_iota(jnp.int32, asked.shape, 0)
    column = lax.broadcasted_iota(jnp.int32, asked.shape, 1)
    short_ref[...] = jnp.sum(jnp.where(row == column, asked, 0), axis=0, keepdims=True)
    to_scalars = pltpu.make_async_copy(short_ref, short, short_sem)
    to_scalars.start()
    to_scalars.wait()

    def put(at, carry):
        placed[at] = geometry_ref[pl.ds(short[0, at], 1), :]
        return carry

    copies = part_copies(placed, place_ref, sems)
    size = placed.shape[0] // PARTS
    for i, copy in enumerate(copies):
        lax.fori_loop(i * size, (i + 1) * size, put, 0, unroll=8)
        copy.start()
    for copy in copies:
        copy.wait()


def place(asked, geometry):
    owners = asked.shape[0]
    return pl.pallas_call(
        place_kernel,
        in_specs=[VMEM_SPEC] * 2,
        out_specs=[HBM_SPEC, VMEM_SPEC],
        out_shape=[
            jax.ShapeDtypeStruct((owners, 1, geometry.shape[1]), jnp.float32),
            jax.ShapeDtypeStruct((1, owners), jnp.int32),
        ],
        scratch_shapes=[
            pltpu.VMEM((owners, 1, geometry.shape[1]), jnp.float32),
            pltpu.SemaphoreType.DMA((PARTS,)),
            pltpu.SMEM((1, owners), jnp.int32),
            pltpu.SemaphoreType.DMA,
        ],
        compiler_params=pltpu.CompilerParams(vmem_limit_bytes=VMEM // 4),
    )(asked, geometry)


def first_kernel(asked_ref, area_ref, emission_ref, ex_out_ref, send_ref, ex, send, ex_sems, send_sems):
    ex[...] = (area_ref[...] * emission_ref[...]).astype(jnp.bfloat16)
    ex_copies = part_copies(ex, ex_out_ref, ex_sems)
    send_copies = part_copies(send, send_ref, send_sems)
    put_asked(asked_ref, ex, send, send_copies)
    for copy in ex_copies:
        copy.start()
    for copy in ex_copies + send_copies:
        copy.wait()


def first(asked, area, emission):
    blocks, hours, block = emission.shape
    owners = asked.shape[0]
    return pl.pallas_call(
        first_kernel,
        in_specs=[SMEM_SPEC] + [VMEM_SPEC] * 2,
        out_specs=[HBM_SPEC] * 2,
        out_shape=[
            pltpu.HBM((blocks, hours, block), jnp.bfloat16),
            pltpu.HBM((owners, hours, block), jnp.bfloat16),
        ],
        scratch_shapes=[
            pltpu.VMEM((blocks, hours, block), jnp.bfloat16),
            pltpu.VMEM((owners, hours, block), jnp.bfloat16),
            pltpu.SemaphoreType.DMA((PARTS,)),
            pltpu.SemaphoreType.DMA((PARTS,)),
        ],
        compiler_params=pltpu.CompilerParams(vmem_limit_bytes=VMEM // 4),
        cost_estimate=pl.CostEstimate(flops=10_000_000, bytes_accessed=8_000_000, transcendentals=0),
    )(asked, area, emission)


def factor_rows(x, y, z, area, facing, near):
    x, y, z = x - 3.0, y - 3.0, z - 3.0
    unit = (math.pi if near else 1.0) / facing
    norm = unit * (x * x + y * y + z * z + area)
    if near:
        terms = (norm, unit, -2.0 * unit * x, -2.0 * unit * y, -2.0 * unit * z)
        order = (0, 0, 1, 1, 0, 2)
    else:
        terms = (unit, norm, unit * x, unit * y, unit * z)
        order = (0, 1, 0, 1, 2, 0)
    found = []
    for term in terms:
        parts = []
        for _ in range(3):
            part = term.astype(jnp.bfloat16).astype(jnp.float32)
            parts.append(part)
            term = term - part
        found += [parts[i] for i in order]
    return found + [jnp.zeros_like(x)] * (FEATURES - len(found))


def factor_blocks(read, count, turned, near, put):
    def group(at, carry):
        for i, feature in enumerate(factor_rows(*read(pl.ds(pl.multiple_of(at * 8, 8), 8)), near)):
            turned[8 * i : 8 * i + 8, :] = feature
        for i in range(8):
            put(at * 8 + i, turned[pl.ds(i, FEATURES, stride=8), :])
        return carry

    lax.fori_loop(0, count // 8, group, 0)


def near_kernel(positions_ref, area_ref, facing_ref, out_ref, geometry_ref, turned, made, sems):
    parts = [positions_ref[i] for i in range(3)] + [area_ref[...], facing_ref[...]]
    for i, part in enumerate(parts):
        geometry_ref[:, i * BLOCK : (i + 1) * BLOCK] = part

    def read(at):
        return [positions_ref[i, at, :] for i in range(3)] + [area_ref[at, :], facing_ref[at, :]]

    def put(at, block):
        made[at] = block.T.astype(jnp.bfloat16)

    factor_blocks(read, made.shape[0], turned, True, put)
    copies = part_copies(made, out_ref, sems)
    for copy in copies:
        copy.start()
    for copy in copies:
        copy.wait()


def far_factors(geometry_ref, out, turned):
    def read(at):
        return [geometry_ref[at, 0, i * BLOCK : (i + 1) * BLOCK] for i in range(5)]

    def put(at, block):
        out[at] = block.astype(jnp.bfloat16)

    factor_blocks(read, out.shape[0], turned, False, put)


def near_factors(positions, patch_area, facing):
    blocks = patch_area.shape[0]
    return pl.pallas_call(
        near_kernel,
        in_specs=[VMEM_SPEC] * 3,
        out_specs=[HBM_SPEC, VMEM_SPEC],
        out_shape=[
            pltpu.HBM((blocks, BLOCK, FEATURES), jnp.bfloat16),
            jax.ShapeDtypeStruct((blocks, 5 * BLOCK), jnp.float32),
        ],
        scratch_shapes=[
            pltpu.VMEM((8 * FEATURES, BLOCK), jnp.float32),
            pltpu.VMEM((blocks, BLOCK, FEATURES), jnp.bfloat16),
            pltpu.SemaphoreType.DMA((PARTS,)),
        ],
        compiler_params=pltpu.CompilerParams(vmem_limit_bytes=VMEM // 4),
        cost_estimate=pl.CostEstimate(flops=10_000_000, bytes_accessed=8_000_000, transcendentals=0),
    )(positions, patch_area, facing)


def local(
    emission, positions, patch_area, facing, albedo_class, albedo_table, fetch_block,
    pair_rows, pair_slots, pair_code,
):
    blocks, hours = emission.shape[:2]
    owners = lax.axis_size("blk")
    core = lax.axis_index("grp")

    def exchange(array):
        return lax.all_to_all(array, "blk", split_axis=0, concat_axis=0, tiled=True)

    def swap(array):
        return lax.ppermute(array, "grp", [(0, 1), (1, 0)])

    asked_rows = exchange(ask(core, fetch_block, owners)).reshape(owners, BLOCK)
    near, own_geometry = near_factors(positions, patch_area, facing)
    placed, asked = place(asked_rows, own_geometry)
    asked = asked.reshape(owners)
    geometry = exchange(placed)

    def words(pair_row, pair_slot, code):
        skip = (pair_slot & 1) ^ core
        return pair_row | (skip << 6) | ((pair_slot >> 1) << 7) | jnp.left_shift(code, 15)

    lists = (pair_rows, pair_slots, pair_code)
    pairs, steps = pair_list(words(*lists), words(*map(swap, lists)))
    area = patch_area[:, None, :]
    exitance, send = first(asked, area, emission)
    send, geometry, near, pairs, steps = lax.optimization_barrier((send, geometry, near, pairs, steps))

    class_ids = jnp.arange(NCLASS, dtype=jnp.int32)
    albedo = jnp.sum(
        jnp.where(albedo_class[..., None] == class_ids, albedo_table, jnp.float32(0.0)), axis=-1
    )[:, None, :]

    fetched = exchange(send)
    tiles, back = build(
        pairs, steps, jnp.asarray(hash_pattern()), near, geometry, exitance, 2 * pair_rows.shape[0]
    )

    asked_other, back = lax.optimization_barrier((swap(asked), back))

    def collect(back, fetched):
        got = exchange(back)
        to_rows = rows(pairs, steps, tiles, fetched, blocks)
        base = emission + albedo * (to_rows[:blocks] + swap(to_rows)[:blocks])
        got, base = lax.optimization_barrier((got, base))
        return own(asked, got, blocks), swap(got), base

    exitance, send = middle(asked, asked_other, *collect(back, fetched), albedo, area)
    fetched = exchange(send)
    back = columns(pairs, steps, tiles, exitance, owners)
    return last(asked_other, *collect(back, fetched), albedo)


def solution(mesh):
    in_specs = (
        P("blk", None, None),
        P(None, "blk", None),
        P("blk", None),
        P("blk", None),
        P("blk", None),
        P(),
        P("blk"),
        P(("blk", "grp")),
        P(("blk", "grp")),
        P(("blk", "grp")),
    )
    out_specs = P("blk", None, None)
    return jax.shard_map(local, mesh=mesh, in_specs=in_specs, out_specs=out_specs, check_vma=False)
```
